32 devices in a mesh: dp: 8 (over y, x, core), seq: 4 (over z).
Axes of the slice: x: 2, y: 2, z: 4, core: 2. Of those that a mesh axis runs over, the one named last changes fastest.
Arguments:
- tokens: bfloat16 [8, 2048, 2048], P('dp', 'seq'), may hold values from -6 to 6
- lengths: int32 [8, 6], P('dp'), may hold values from 1 to 1537, as said below
- gain_one: float32 [2048], P(('dp', 'seq')), may hold values from 0.5 to 1.5
- w_query: float32 [2048, 2048], P(('dp', 'seq')), may hold values from -0.125 to 0.125
- w_key: float32 [2048, 128], P(('dp', 'seq')), may hold values from -0.125 to 0.125
- w_value: float32 [2048, 128], P(('dp', 'seq')), may hold values from -0.125 to 0.125
- w_out: float32 [2048, 2048], P(('dp', 'seq')), may hold values from -1.5 to 1.5
- gain_two: float32 [2048], P(('dp', 'seq')), may hold values from 0.5 to 1.5
- w_gate: float32 [2048, 5632], P(('dp', 'seq')), may hold values from -0.125 to 0.125
- w_up: float32 [2048, 5632], P(('dp', 'seq')), may hold values from -0.125 to 0.125
- w_down: float32 [5632, 2048], P(('dp', 'seq')), may hold values from -0.078125 to 0.078125
- cotangent: bfloat16 [8, 2048, 2048], P('dp', 'seq'), may hold values from -6 to 6
Outputs:
- output: bfloat16 [8, 2048, 2048], P('dp', 'seq')
- tokens_grad: bfloat16 [8, 2048, 2048], P('dp', 'seq')
- gain_one_grad: float32 [2048], P(('dp', 'seq'))
- w_query_grad: float32 [2048, 2048], P(('dp', 'seq'))
- w_key_grad: float32 [2048, 128], P(('dp', 'seq'))
- w_value_grad: float32 [2048, 128], P(('dp', 'seq'))
- w_out_grad: float32 [2048, 2048], P(('dp', 'seq'))
- gain_two_grad: float32 [2048], P(('dp', 'seq'))
- w_gate_grad: float32 [2048, 5632], P(('dp', 'seq'))
- w_up_grad: float32 [2048, 5632], P(('dp', 'seq'))
- w_down_grad: float32 [5632, 2048], P(('dp', 'seq'))
The draws below stay inside these ranges and needn't reach their ends.
Inputs may be any that keep to these rules, and one draw needn't show every extreme that they name: Each row's lengths sum to 2048.
All inputs are finite; a program needn't handle non-finite values.
Results may differ from the reference program's by a relative error of at most 0.014.
The reference program's roundings to bfloat16 on the way count: a program that leaves them out, or rounds other values in their place, can miss the bound.
Values may be sent and summed in bfloat16 or wider, within the bound.
A program may use at most 384 MiB of HBM per device.

```python
import math
import jax
import jax.numpy as jnp
from jax import lax

D = 2048
HEADS = 16
HEAD = 128
FF = 5632
WINDOW = 512
LENGTH = 2048
DOCS = 6
SEQS = 8
GROUP = 512


def draw_lengths(key, part):
    key = jax.random.fold_in(key, 11)

    def one_row(row_key):
        cut_key, place_key = jax.random.split(row_key, 2)
        order = jax.random.permutation(cut_key, GROUP - 2) + 1
        cuts = jnp.sort(order[:DOCS - 2]).astype(jnp.int32)
        edges = jnp.concatenate([jnp.zeros((1,), jnp.int32), cuts, jnp.full((1,), GROUP - 1, jnp.int32)])
        others = edges[1:] - edges[:-1]
        spot = jax.random.randint(place_key, (), 0, DOCS)
        slots = jnp.arange(DOCS, dtype=jnp.int32)
        before = others[jnp.clip(slots, 0, DOCS - 2)]
        after = others[jnp.clip(slots - 1, 0, DOCS - 2)]
        longest = jnp.full((DOCS,), LENGTH - GROUP + 1, jnp.int32)
        return jnp.where(slots < spot, before, jnp.where(slots == spot, longest, after)).astype(jnp.int32)
    return jax.vmap(one_row)(jax.random.split(key, SEQS))


def levels(rng, dims, pieces, least, largest):
    loudness = 1.0
    for dim, shards_of in pieces:
        steps = jax.random.uniform(jax.random.fold_in(jax.random.fold_in(rng, 6), dim), (shards_of,), jnp.float32, least / len(pieces), largest / len(pieces))
        loudness = loudness * jnp.repeat(jnp.exp(steps), dims[dim] // shards_of).reshape((-1,) + (1,) * (len(dims) - 1 - dim))
    return loudness


def gaussian(key, dims, deviation, most, pieces=(), kind=jnp.bfloat16):
    gain = levels(key, dims, pieces, -0.22, 0.18) if pieces else 1.0
    result = jax.random.normal(key, dims, jnp.float32) * deviation * gain
    return jnp.minimum(jnp.maximum(result, -most), most).astype(kind)


def setup_inputs(seed: int = 0) -> dict:
    seeds = jax.random.split(jax.random.key(seed), 13)
    return {
        "tokens": gaussian(seeds[0], (SEQS, LENGTH, D), 1.0, 6.0, ((0, 8), (1, 4))),
        "lengths": draw_lengths(jax.random.fold_in(seeds[12], 71), 0),
        "gain_one": jnp.clip(1.0 + 0.1 * jax.random.normal(seeds[2], (D,), jnp.float32), 0.5, 1.5),
        "w_query": gaussian(seeds[3], (D, HEADS * HEAD), D ** -0.5, 0.125, ((0, 32),), jnp.float32),
        "w_key": gaussian(seeds[4], (D, HEAD), D ** -0.5, 0.125, ((0, 32),), jnp.float32),
        "w_value": gaussian(seeds[5], (D, HEAD), D ** -0.5, 0.125, ((0, 32),), jnp.float32),
        "w_out": gaussian(seeds[6], (HEADS * HEAD, D), (HEADS * HEAD // 128) ** -0.5, 1.5, ((0, 32),), jnp.float32),
        "gain_two": jnp.clip(1.0 + 0.1 * jax.random.normal(seeds[7], (D,), jnp.float32), 0.5, 1.5),
        "w_gate": gaussian(seeds[8], (D, FF), D ** -0.5, 0.125, ((0, 32),), jnp.float32),
        "w_up": gaussian(seeds[9], (D, FF), D ** -0.5, 0.125, ((0, 32),), jnp.float32),
        "w_down": gaussian(seeds[10], (FF, D), FF ** -0.5, 0.078125, ((0, 32),), jnp.float32),
        "cotangent": gaussian(seeds[11], (SEQS, LENGTH, D), 1.0, 6.0, ((0, 8), (1, 4))),
    }


EPS = 1e-05
HIGH = lax.Precision.HIGHEST

@jax.custom_vjp
def low(v):
    return lax.optimization_barrier(v.astype(jnp.bfloat16)).astype(jnp.float32)

@jax.custom_vjp
def low_back(v):
    return v

def low_keep(v):
    return (low(v), None)

def low_pass(kept, grad):
    return (grad,)

def back_keep(v):
    return (v, None)

def back_low(kept, grad):
    return (low(grad),)
low.defvjp(low_keep, low_pass)
low_back.defvjp(back_keep, back_low)

def product(left, right):
    return jnp.dot(left, right, preferred_element_type=jnp.float32, precision=HIGH)

def documents(doc_lengths, index):
    ends = jnp.cumsum(doc_lengths, axis=-1).astype(jnp.int32)
    passed = (index[None, :, None] >= ends[:, None, :]).astype(jnp.int32)
    segment = lax.optimization_barrier(jnp.sum(passed, axis=-1)).astype(jnp.int32)
    before = lax.optimization_barrier(jnp.sum(passed * doc_lengths[:, None, :], axis=-1)).astype(jnp.int32)
    return (segment, (index[None, :] - before).astype(jnp.int32))

def rope_tables(position):
    half = HEAD // 2
    freq = jnp.exp(jnp.arange(half, dtype=jnp.float32) * (-2.0 * math.log(10000.0) / HEAD))
    angles = position.astype(jnp.float32)[..., None] * freq
    return (jnp.cos(angles), jnp.sin(angles))

def rotate(vec, cosine, sine):
    half = vec.shape[-1] // 2
    first = vec[..., :half]
    second = vec[..., half:]
    return jnp.concatenate([first * cosine - second * sine, second * cosine + first * sine], axis=-1)

def forward(rows, gain_one, w_query, w_key, w_value, w_out, gain_two, w_gate, w_up, w_down, segment, position):
    length = rows.shape[0]
    scale_one = lax.rsqrt(lax.optimization_barrier(jnp.mean(rows * rows, axis=-1, keepdims=True)) + EPS)
    normed = low(rows * scale_one * low(gain_one))
    query = low_back(product(normed, low(w_query)))
    key = low_back(product(normed, low(w_key)))
    value = low(low_back(product(normed, low(w_value))))
    cosine, sine = rope_tables(position)
    query_turned = low(rotate(query.reshape(length, HEADS, HEAD), cosine[:, None, :], sine[:, None, :]))
    key_turned = low(rotate(key, cosine, sine))
    block = min(512, length)
    starts = jnp.arange(length // block, dtype=jnp.int32) * block

    def attend(start):
        picked = lax.dynamic_slice_in_dim(query_turned, start, block, 0)
        raw = jnp.einsum('qhe,ke->hqk', picked, key_turned, precision=HIGH)
        scores = low_back(raw * (1.0 / math.sqrt(HEAD)))
        rows_at = start + jnp.arange(block, dtype=jnp.int32)
        cols_at = jnp.arange(length, dtype=jnp.int32)
        near = (rows_at[:, None] >= cols_at[None, :]) & (rows_at[:, None] - cols_at[None, :] < WINDOW)
        same = lax.dynamic_slice_in_dim(segment, start, block, 0)[:, None] == segment[None, :]
        scores = jnp.where((near & same)[None], scores, -1e+30)
        top = lax.optimization_barrier(jnp.max(scores, axis=-1, keepdims=True))
        weight = jnp.exp(scores - top)
        prob = low(weight / lax.optimization_barrier(jnp.sum(weight, axis=-1, keepdims=True)))
        return jnp.einsum('hqk,ke->qhe', prob, value, precision=HIGH)
    mixed = lax.map(jax.checkpoint(attend), starts).reshape(length, HEADS * HEAD)
    mixed = low(low_back(mixed))
    mid = rows + low_back(product(mixed, low(w_out)))
    scale_two = lax.rsqrt(lax.optimization_barrier(jnp.mean(mid * mid, axis=-1, keepdims=True)) + EPS)
    normed_two = low(mid * scale_two * low(gain_two))
    gate = low_back(product(normed_two, low(w_gate)))
    up_val = low_back(product(normed_two, low(w_up)))
    hidden = low(jax.nn.silu(gate) * up_val)
    return mid + product(hidden, low(w_down))

def reference(tokens, lengths, gain_one, w_query, w_key, w_value, w_out, gain_two, w_gate, w_up, w_down, cotangent):
    weights = (gain_one, w_query, w_key, w_value, w_out, gain_two, w_gate, w_up, w_down)
    index = jnp.arange(LENGTH, dtype=jnp.int32)

    def one(totals, item):
        rows, doc_lengths, cot = item
        segment, position = documents(doc_lengths[None, :], index)

        def run(rows_f, *params):
            return forward(rows_f, *params, segment[0], position[0])
        out, pull = jax.vjp(run, rows.astype(jnp.float32), *weights)
        grads = pull(cot.astype(jnp.float32))
        totals = tuple((t + g for t, g in zip(totals, grads[1:])))
        return (totals, (out.astype(jnp.bfloat16), grads[0].astype(jnp.bfloat16)))
    zeros = tuple((jnp.zeros(w.shape, jnp.float32) for w in weights))
    totals, (outs, backs) = lax.scan(one, zeros, (tokens, lengths, cotangent))
    return (outs, backs, totals[0], totals[1], totals[2], totals[3], totals[4], totals[5], totals[6], totals[7], totals[8])
```

```python
import functools
import math

import jax
import jax.numpy as jnp
from jax import lax
from jax.experimental import pallas as pl
from jax.experimental.pallas import tpu as pltpu
from jax.sharding import PartitionSpec as P

HEADS = 16
HEAD = 128
WINDOW = 512


EPS = 1e-05


def shifted(value, axis, steps):
    count = lax.axis_size(axis)
    initial, last = (max(0, -steps), min(count, count - steps))
    return lax.ppermute(value, axis, [(source, source + steps) for source in range(initial, last)])


def documents(doc_lengths, index):
    ends = jnp.cumsum(doc_lengths, axis=-1)
    passed = (index[None, :, None] >= ends[:, None, :]).astype(jnp.int32)
    segment = jnp.sum(passed, axis=-1)
    before = jnp.sum(passed * doc_lengths[:, None, :], axis=-1)
    return (segment, index[None, :] - before)


def rope_tables(position):
    half = HEAD // 2
    freq = jnp.exp(jnp.arange(half, dtype=jnp.float32) * (-2.0 * math.log(10000.0) / HEAD))
    angles = position.astype(jnp.float32)[..., None] * freq
    return (jnp.cos(angles), jnp.sin(angles))


def rotate(vec, cosine, sine):
    half = vec.shape[-1] // 2
    first = vec[..., :half]
    second = vec[..., half:]
    return jnp.concatenate(
        [first * cosine - second * sine, second * cosine + first * sine], axis=-1
    )


def norm_back(grad_normed, rows, scale, gain):
    inner = grad_normed * gain
    grad_gain = jnp.sum(grad_normed * rows * scale, axis=0)
    grad_rows = scale * inner - rows * (scale * scale * scale) * jnp.mean(
        inner * rows, axis=-1, keepdims=True
    )
    return (grad_rows, grad_gain)


def matmul(left, right):
    return jnp.dot(left, right, preferred_element_type=jnp.float32)


def after(values, *others):
    return lax.optimization_barrier((values, others))[0]


def partner(value, bit):
    count = lax.axis_size("dp")
    return lax.ppermute(value, "dp", [(source, source ^ (1 << bit)) for source in range(count)])


def around(value, steps):
    count = lax.axis_size("seq")
    return lax.ppermute(
        value, "seq", [(source, (source + steps) % count) for source in range(count)]
    )


def dp_bits():
    return lax.axis_size("dp").bit_length() - 1


MIB = 1 << 20
ANYWHERE = pl.BlockSpec(memory_space=pl.ANY)


def kernel_params(flops, traffic):
    return {
        "compiler_params": pltpu.CompilerParams(vmem_limit_bytes=58 * MIB),
        "cost_estimate": pl.CostEstimate(flops=flops, bytes_accessed=traffic, transcendentals=0),
    }


def owner(number):
    return lax.bitwise_xor(lax.axis_index("dp"), number)


def rows_kernel(count, gained, near, left, *refs):
    pieces, rest = refs[:count], refs[count:]
    if gained:
        out, normed, gains, held, sems = rest
    else:
        out, held, sems = rest
    step = pl.program_id(0)
    rows, columns = held.shape[1], out.shape[1]
    copies = [
        pltpu.make_async_copy(piece, held.at[number], sems.at[number])
        for number, piece in enumerate(pieces)
    ]

    @pl.when(step == 0)
    def _():
        for copy in copies:
            copy.start()

    for number, copy in enumerate(copies):

        @pl.when(step == number)
        def _(copy=copy):
            copy.wait()

    start = pl.multiple_of(owner(step) * rows, rows)
    block = left[:, pl.ds(start, rows)]
    if gained:
        turned = held[step, :, columns:].astype(jnp.float32).T
        gains[...] = turned[:8]
        block = (block * turned[:1]).astype(normed.dtype)
        normed[...] = block
    part = matmul(block, held[step, :, :columns])

    @pl.when(step == 0)
    def _():
        out[...] = part

    @pl.when(step > 0)
    def _():
        out[...] += part


def near_places(count):
    return lax.bitwise_xor(lax.axis_index("dp"), jnp.arange(count, dtype=jnp.int32))


def by_rows(left, held, columns):
    count, (rows, wide) = len(held), held[0].shape
    tokens = left.shape[0]
    gained = wide > columns
    out_shape = [jax.ShapeDtypeStruct((tokens, columns), jnp.float32)]
    out_specs = [pl.BlockSpec((tokens, columns), lambda step, near: (0, 0))]
    if gained:
        out_shape += [
            jax.ShapeDtypeStruct(left.shape, held[0].dtype),
            jax.ShapeDtypeStruct((8, left.shape[1]), jnp.float32),
        ]
        out_specs += [
            pl.BlockSpec((tokens, rows), lambda step, near: (0, near[step])),
            pl.BlockSpec((8, rows), lambda step, near: (0, near[step])),
        ]
    return pl.pallas_call(
        functools.partial(rows_kernel, count, gained),
        out_shape=out_shape,
        grid_spec=pltpu.PrefetchScalarGridSpec(
            num_scalar_prefetch=1,
            grid=(count,),
            in_specs=[pl.BlockSpec(left.shape, lambda step, near: (0, 0))] + [ANYWHERE] * count,
            out_specs=out_specs,
            scratch_shapes=[
                pltpu.VMEM((count, rows, wide), held[0].dtype),
                pltpu.SemaphoreType.DMA((count,)),
            ],
        ),
        **kernel_params(2 * tokens * count * rows * columns, 2 * count * rows * columns),
    )(near_places(count), left, *[held[place] for place in range(count)])


def back_kernel(count, many, near, *refs):
    lefts = refs[:many]
    pieces = refs[many : many + many * count]
    out, held, sems = refs[many + many * count :]
    step = pl.program_id(0)

    def copy(number, which, slot):
        return pltpu.make_async_copy(
            pieces[which * count + number], held.at[slot, which], sems.at[slot, which]
        )

    for number in range(count):

        @pl.when(step == max(number - 1, 0))
        def _(number=number):
            for which in range(many):
                copy(number, which, number % 2).start()

    slot = lax.rem(step, 2)
    total = None
    for which in range(many):
        copy(0, which, slot).wait()
        part = lax.dot_general(
            lefts[which][...],
            held[slot, which, :, : lefts[which].shape[1]],
            (((1,), (1,)), ((), ())),
            preferred_element_type=jnp.float32,
        )
        total = part if total is None else total + part
    out[...] = total.astype(out.dtype)


def back_by_rows(lefts, helds, dtype):
    count, many = len(helds[0]), len(lefts)
    rows, wide = helds[0][0].shape
    tokens, columns = lefts[0].shape
    near = near_places(count)
    return pl.pallas_call(
        functools.partial(back_kernel, count, many),
        out_shape=jax.ShapeDtypeStruct((tokens, count * rows), dtype),
        grid_spec=pltpu.PrefetchScalarGridSpec(
            num_scalar_prefetch=1,
            grid=(count,),
            in_specs=[pl.BlockSpec((tokens, columns), lambda step, near: (0, 0))] * many
            + [ANYWHERE] * (many * count),
            out_specs=pl.BlockSpec((tokens, rows), lambda step, near: (0, near[step])),
            scratch_shapes=[
                pltpu.VMEM((2, many, rows, wide), helds[0][0].dtype),
                pltpu.SemaphoreType.DMA((2, many)),
            ],
        ),
        **kernel_params(
            2 * tokens * many * count * rows * columns, 2 * many * count * rows * columns
        ),
    )(near, *lefts, *[held[place] for held in helds for place in range(count)])


def gate_kernel(count, left, *refs):
    pieces = refs[: 2 * count]
    gate, up, hidden, turned, held, sems = refs[2 * count :]
    step, steps = pl.program_id(0), pl.num_programs(0)
    rows, tile = pieces[0].shape[0], gate.shape[1]

    def copies(number, slot):
        column = pl.multiple_of(number * tile, tile)
        for which in range(2):
            for place in range(count):
                start = pl.multiple_of(owner(place) * rows, rows)
                yield pltpu.make_async_copy(
                    pieces[which * count + place].at[:, pl.ds(column, tile)],
                    held.at[slot, which, pl.ds(start, rows), :],
                    sems.at[slot, which, place],
                )

    @pl.when(step == 0)
    def _():
        for copy in copies(0, 0):
            copy.start()

    @pl.when(step + 1 < steps)
    def _():
        for copy in copies(step + 1, lax.rem(step + 1, 2)):
            copy.start()

    slot = lax.rem(step, 2)
    for copy in copies(step, slot):
        copy.wait()
    gate_tile = matmul(left[...], held[slot, 0])
    gate[...] = gate_tile
    up_tile = matmul(left[...], held[slot, 1])
    up[...] = up_tile
    value = (gate_tile * jax.nn.sigmoid(gate_tile) * up_tile).astype(hidden.dtype)
    hidden[...] = value
    turned[...] = value.T


def gate_up(left, gates, ups):
    count, (rows, columns) = len(gates), gates[0].shape
    tokens = left.shape[0]
    tile = next(size for size in (512, 256, 128) if columns % size == 0)
    across = pl.BlockSpec((tokens, tile), lambda step: (0, step))
    return pl.pallas_call(
        functools.partial(gate_kernel, count),
        out_shape=[
            jax.ShapeDtypeStruct((tokens, columns), jnp.float32),
            jax.ShapeDtypeStruct((tokens, columns), jnp.float32),
            jax.ShapeDtypeStruct((tokens, columns), left.dtype),
            jax.ShapeDtypeStruct((columns, tokens), left.dtype),
        ],
        grid=(columns // tile,),
        in_specs=[pl.BlockSpec(left.shape, lambda step: (0, 0))] + [ANYWHERE] * (2 * count),
        out_specs=[across, across, across, pl.BlockSpec((tile, tokens), lambda step: (step, 0))],
        scratch_shapes=[
            pltpu.VMEM((2, 2, count * rows, tile), left.dtype),
            pltpu.SemaphoreType.DMA((2, 2, count)),
        ],
        **kernel_params(
            4 * tokens * count * rows * columns, 4 * columns * (count * rows + 3 * tokens)
        ),
    )(left, *[held[place] for held in (gates, ups) for place in range(count)])


def down_kernel(count, together, near, hidden, gate, up, cot, mid, *refs):
    pieces = refs[: 2 * count]
    output, grad_gate, grad_up, held, total, sems = refs[2 * count :]
    step, steps = pl.program_id(0), pl.num_programs(0)
    rows, side = pieces[0].shape

    def copies(number, slot):
        for part in range(together):
            spot = lax.rem(owner(part), together)
            start = pl.multiple_of(spot * rows, rows)
            for which in range(2):
                yield pltpu.make_async_copy(
                    pieces[which * count + number * together + part],
                    held.at[slot, pl.ds(start, rows), which * side : (which + 1) * side],
                    sems.at[slot, part, which],
                )

    for number in range(count // together):

        @pl.when(step == max(number - 1, 0))
        def _(number=number):
            for copy in copies(number, number % 2):
                copy.start()

    slot = lax.rem(step, 2)
    for copy in copies(0, slot):
        copy.wait()
    chunk = 128

    @pl.loop(0, cot.shape[0] // chunk)
    def _(index):
        start = pl.ds(pl.multiple_of(index * chunk, chunk), chunk)
        weight = held[slot]
        grad = lax.dot_general(
            cot[start, :], weight, (((1,), (1,)), ((), ())), preferred_element_type=jnp.float32
        )
        gate_rows, up_rows = gate[start, :], up[start, :]
        sigma = jax.nn.sigmoid(gate_rows)
        grad_up[start, :] = (grad * (gate_rows * sigma)).astype(grad_up.dtype)
        grad_gate[start, :] = (
            grad * up_rows * (sigma * (1.0 + gate_rows * (1.0 - sigma)))
        ).astype(grad_gate.dtype)
        added = matmul(hidden[start, :], weight)

        @pl.when(step == 0)
        def _():
            total[start, :] = mid[start, :] + added

        @pl.when(step > 0)
        def _():
            total[start, :] += added

    @pl.when(step == steps - 1)
    def _():
        output[...] = total[...].astype(output.dtype)


def down_and_back(hidden, gate, up, cot, mid, helds):
    count, (rows, side) = len(helds[0]), helds[0][0].shape
    tokens, width = cot.shape
    together = next(size for size in (1, 2, 4, 8, 16) if size * rows % 128 == 0)
    tile = together * rows
    dp = lax.axis_index("dp")
    near = lax.bitwise_xor(
        lax.div(dp, together), jnp.arange(count // together, dtype=jnp.int32)
    )
    across = pl.BlockSpec((tokens, tile), lambda step, near: (0, near[step]))

    def fixed(size):
        return pl.BlockSpec((tokens, size), lambda step, near: (0, 0))

    columns = count * rows
    return pl.pallas_call(
        functools.partial(down_kernel, count, together),
        out_shape=[
            jax.ShapeDtypeStruct((tokens, width), jnp.bfloat16),
            jax.ShapeDtypeStruct((tokens, columns), jnp.bfloat16),
            jax.ShapeDtypeStruct((tokens, columns), jnp.bfloat16),
        ],
        grid_spec=pltpu.PrefetchScalarGridSpec(
            num_scalar_prefetch=1,
            grid=(count // together,),
            in_specs=[across, across, across, fixed(width), fixed(width)]
            + [ANYWHERE] * (2 * count),
            out_specs=[fixed(width), across, across],
            scratch_shapes=[
                pltpu.VMEM((2, tile, width), hidden.dtype),
                pltpu.VMEM((tokens, width), jnp.float32),
                pltpu.SemaphoreType.DMA((2, together, 2)),
            ],
        ),
        **kernel_params(4 * tokens * width * columns, 2 * columns * (width + 7 * tokens)),
    )(
        near, hidden, gate, up, cot, mid,
        *[held[place] for held in helds for place in range(count)],
    )


class Flow:
    def __init__(self):
        self.ended = []

    def round(self, moves):
        values = after([value for value, _ in moves], self.ended)
        got = [partner(value, bit) for value, (_, bit) in zip(values, moves)]
        self.ended = list(got)
        return got

    def holds(self, *results):
        self.ended.extend(results)


class Spreads:
    def __init__(self, order):
        self.order, self.helds = order, [{}, {}]

    def direct(self, flow, number, line, also=()):
        held = self.helds[number]
        held[0] = line
        moves = [(line, 0)] + [(line, bit) for bit in self.order] + list(also)
        got = flow.round(moves)
        held[1] = got[0]
        for bit, piece in zip(self.order, got[1:]):
            held[1 << bit] = piece
        return got[1 + len(self.order) :]

    def double(self):
        return [
            (number, place)
            for number, held in enumerate(self.helds)
            for place in sorted(held)
            if not place & 1 and place | 1 not in held
        ]

    def moves(self, names):
        return [(self.helds[number][place], 0) for number, place in names]

    def put(self, names, got):
        for (number, place), piece in zip(names, got):
            self.helds[number][place | 1] = piece

    def cross(self, flow, level, also):
        names, targets, moves = self.double(), [], []
        for number, turn in enumerate((self.order, self.order[::-1])):
            for place in range(2 << len(self.order)):
                bits = [bit for bit in turn if place >> bit & 1]
                if not place & 1 and len(bits) == level:
                    targets.append((number, place))
                    moves.append((self.helds[number][place ^ (1 << bits[-1])], bits[-1]))
        got = flow.round(moves + self.moves(names) + list(also))
        for (number, place), piece in zip(targets, got):
            self.helds[number][place] = piece
        end = len(targets) + len(names)
        self.put(names, got[len(targets) : end])
        return got[end:]

    def crosses(self, flow, also=()):
        extra = []
        for level in range(2, len(self.order) + 1):
            extra += self.cross(flow, level, also if level == 2 else ())
        return extra


def places_of(order):
    places = [0]
    for bit in reversed(order):
        places = places + [place | (1 << bit) for place in places]
    return places


def arranged(turned, order):
    dp, me = lax.axis_size("dp"), lax.axis_index("dp")
    block = turned.shape[0] // dp
    return jnp.concatenate(
        [
            lax.dynamic_slice_in_dim(turned, lax.bitwise_xor(me, place) * block, block, 0)
            for place in places_of(order)
        ],
        axis=0,
    )


class Scattered:
    def __init__(self, turned, right, order):
        self.lhs, self.right, self.order = arranged(turned, order), right, order
        self.arrived, self.step = [], 0

    def total(self, rows, parts):
        total = matmul(rows, self.right)
        for part in parts:
            total = total + part.astype(jnp.float32)
        return total

    def send(self):
        half = self.lhs.shape[0] // 2
        sent = self.total(self.lhs[half:], [part[half:] for part in self.arrived])
        self.sent = sent.astype(jnp.bfloat16)
        self.lhs = self.lhs[:half]
        self.arrived = [part[:half] for part in self.arrived]
        return self.sent

    def move(self):
        return (self.sent, self.order[self.step])

    def receive(self, got):
        self.arrived.append(got)
        self.step += 1

    def line(self):
        self.sent = self.total(self.lhs, self.arrived).astype(jnp.bfloat16)
        return self.sent


def finish(jobs):
    sent = jnp.concatenate([job.sent for job in jobs], axis=1)
    return lax.psum_scatter(sent, "seq", scatter_dimension=0, tiled=True).astype(jnp.float32)


def on_device(
    tokens,
    lengths,
    gain_one,
    w_query,
    w_key,
    w_value,
    w_out,
    gain_two,
    w_gate,
    w_up,
    w_down,
    cotangent,
):
    half_type = jnp.bfloat16
    batch, group, width = tokens.shape
    count = batch * group
    upper = tuple(range(1, dp_bits()))
    inner = w_query.shape[1]
    middle = w_down.shape[1] // 2

    def along(shard):
        return lax.all_gather(shard, "seq", axis=0, tiled=True)

    gains = jnp.stack([gain_one, gain_two], axis=1)
    first = jnp.concatenate(
        [w_query, w_key, w_value, jnp.pad(gains, ((0, 0), (0, HEAD - 2)))], axis=1
    ).astype(half_type)
    columns_first = inner + 2 * HEAD
    flow = Flow()
    line_first = along(first)
    line_out = along(after(w_out.astype(half_type), line_first))
    line_gate = along(after(w_gate.astype(half_type), line_out))
    line_up = along(after(w_up.astype(half_type), line_gate))
    down_half = w_down.astype(half_type)
    line_left = along(after(down_half[:, :middle], line_up))
    line_right = along(after(down_half[:, middle:], line_left))
    one_spread, two_spread, three_spread = Spreads(upper), Spreads(upper), Spreads(upper)
    one_spread.direct(flow, 0, line_first)
    flow.holds(line_out)
    one_spread.direct(flow, 1, line_out)
    one_spread.crosses(flow)
    flow.holds(line_gate)
    left_over = one_spread.double()
    got = two_spread.direct(flow, 0, line_gate, one_spread.moves(left_over))
    one_spread.put(left_over, got)
    full_one = one_spread.helds

    reach = (WINDOW - 2) // group + 1
    offset = lax.axis_index("seq") * group
    query_at = offset + jnp.arange(group, dtype=jnp.int32)
    key_at = offset - reach * group + jnp.arange((reach + 1) * group, dtype=jnp.int32)
    query_seg, query_pos = documents(lengths, query_at)
    key_seg = documents(lengths, key_at)[0]
    allowed = (
        (key_at[None, :] >= 0)
        & (query_at[:, None] >= key_at[None, :])
        & (query_at[:, None] - key_at[None, :] < WINDOW)
    )
    allowed = (allowed[None] & (query_seg[:, :, None] == key_seg[:, None, :]))[:, None]
    cosine, sine = rope_tables(query_pos)
    factor = 1.0 / math.sqrt(HEAD)
    rows = tokens.astype(jnp.float32).reshape(count, width)
    scale_one = lax.rsqrt(jnp.mean(rows * rows, axis=-1, keepdims=True) + EPS)
    mapped, normed, gain_rows = by_rows(rows * scale_one, full_one[0], columns_first)
    gain_a, gain_b = gain_rows[0], gain_rows[1]
    query = mapped[:, :inner].reshape(batch, group, HEADS, HEAD)
    key = mapped[:, inner : inner + HEAD].reshape(batch, group, HEAD)
    value = mapped[:, inner + HEAD :].astype(half_type).reshape(batch, group, HEAD)
    query_turned = rotate(query, cosine[:, :, None, :], sine[:, :, None, :]).astype(half_type)
    key_turned = rotate(key, cosine, sine).astype(half_type)
    paired = jnp.concatenate([key_turned, value], axis=-1)
    pieces = []
    for step in range(reach, 0, -1):
        pieces.append(shifted(paired, "seq", step))
    pieces.append(paired)
    seen = jnp.concatenate(pieces, axis=1)
    keys_seen = seen[..., :HEAD]
    values_seen = seen[..., HEAD:]

    def scores_of():
        raw = jnp.einsum(
            "bqhe,bke->bhqk", query_turned, keys_seen, preferred_element_type=jnp.float32
        )
        return jnp.where(allowed, raw * factor, -1e30)

    scores = scores_of()
    flow.holds(line_up, query_turned)
    two_spread.direct(flow, 1, line_up)
    top = jnp.max(scores, axis=-1, keepdims=True)
    weight = jnp.exp(scores - top)
    total = jnp.sum(weight, axis=-1, keepdims=True)
    log_total = top + jnp.log(total)
    probs = (weight / total).astype(half_type)
    mixed = jnp.einsum("bhqk,bke->bqhe", probs, values_seen, preferred_element_type=jnp.float32)
    mixed = mixed.astype(half_type).reshape(count, HEADS * HEAD)
    mid = rows + by_rows(mixed, full_one[1], width)[0]
    scale_two = lax.rsqrt(jnp.mean(mid * mid, axis=-1, keepdims=True) + EPS)
    normed_two = (mid * scale_two * gain_b).astype(half_type)

    flow.holds(normed_two, line_left)
    two_spread.crosses(flow)
    flow.holds(line_right)
    left_over = two_spread.double()
    got = three_spread.direct(flow, 0, line_left, two_spread.moves(left_over))
    two_spread.put(left_over, got)
    full_two = two_spread.helds
    gate, up_val, hidden, hidden_turned = gate_up(normed_two, *full_two)

    grad_out = cotangent.reshape(count, width)
    orders = ((0,) + upper, (0,) + upper[::-1])
    three = [
        Scattered(hidden_turned, grad_out[:, :middle], orders[0]),
        Scattered(hidden_turned, grad_out[:, middle:], orders[1]),
    ]

    def send(jobs):
        return [job.send() for job in jobs]

    three_spread.direct(flow, 1, line_right)
    flow.holds(*send(three))
    got = three_spread.crosses(flow, [job.move() for job in three])
    for job, piece in zip(three, got):
        job.receive(piece)
    send(three)
    left_over = three_spread.double()

    def exchange(jobs, also=()):
        got = flow.round([job.move() for job in jobs] + list(also))
        for job, piece in zip(jobs, got):
            job.receive(piece)
        return got[len(jobs) :]

    got = exchange(three, three_spread.moves(left_over))
    three_spread.put(left_over, got)
    full_three = three_spread.helds
    output, grad_gate, grad_up = down_and_back(hidden, gate, up_val, grad_out, mid, full_three)
    output = output.reshape(batch, group, width)
    turned_two = normed_two.T
    two = [Scattered(turned_two, grad_gate, orders[0]), Scattered(turned_two, grad_up, orders[1])]
    flow.holds(*send(two))
    for step in range(len(upper) - 1):
        send(three)
        if step == 0:
            got = exchange(three, [job.move() for job in two])
            for job, piece in zip(two, got):
                job.receive(piece)
        else:
            exchange(three)
    done = [job.line() for job in three]
    sent = send(two)
    grad_gate, grad_up = after((grad_gate, grad_up), sent, done)
    exchange(two)
    down_done = finish(three)
    grad_normed_two = back_by_rows([grad_gate, grad_up], full_two, jnp.float32)
    back_mid, gain_two_term = norm_back(grad_normed_two, mid, scale_two, gain_b)
    grad_mid = grad_out.astype(jnp.float32) + back_mid
    grad_branch = grad_mid.astype(half_type)
    one_b = Scattered(mixed.T, grad_branch, orders[1])
    sent = one_b.send()
    grad_branch = after(grad_branch, sent)
    grad_mixed = back_by_rows([grad_branch], full_one[1:], half_type).reshape(batch, group, HEADS, HEAD)
    probs_full = jnp.exp(scores_of() - log_total)
    grad_probs = jnp.einsum(
        "bqhe,bke->bhqk", grad_mixed, values_seen, preferred_element_type=jnp.float32
    )
    grad_values = jnp.einsum(
        "bhqk,bqhe->bke", probs, grad_mixed, preferred_element_type=jnp.float32
    )
    centre = jnp.sum(probs_full * grad_probs, axis=-1, keepdims=True)
    grad_scores = (probs_full * (grad_probs - centre)).astype(half_type)
    flow.holds(grad_scores)
    for step in range(len(upper) - 1):
        sent = send(two)
        grad_scores = after(grad_scores, sent)
        if step == 0:
            one_b.receive(exchange(two, [one_b.move()])[0])
        else:
            exchange(two)
    grad_query = (
        jnp.einsum("bhqk,bke->bqhe", grad_scores, keys_seen, preferred_element_type=jnp.float32)
        * factor
    )
    grad_keys = (
        jnp.einsum("bhqk,bqhe->bke", grad_scores, query_turned, preferred_element_type=jnp.float32)
        * factor
    )
    grad_seen = jnp.concatenate([grad_keys, grad_values], axis=-1)
    own = grad_seen[:, reach * group :]
    for step in range(1, reach + 1):
        part = grad_seen[:, (reach - step) * group : (reach - step + 1) * group]
        own = own + shifted(part.astype(jnp.bfloat16), "seq", -step).astype(part.dtype)
    grad_key = rotate(own[..., :HEAD], cosine, -sine).astype(half_type).reshape(count, HEAD)
    grad_value = own[..., HEAD:].astype(half_type).reshape(count, HEAD)
    grad_q = (
        rotate(grad_query, cosine[:, :, None, :], -sine[:, :, None, :])
        .astype(half_type)
        .reshape(count, HEADS * HEAD)
    )
    grad_first = jnp.concatenate([grad_q, grad_key, grad_value], axis=1)
    one_a = Scattered(normed.T, grad_first, orders[0])
    sent = one_a.send()
    one = [one_a, one_b]
    done = [job.line() for job in two]
    gate_done, up_done = [finish([job]) for job in two]
    grad_first = after(grad_first, sent, done)
    grad_normed = back_by_rows([grad_first], full_one[:1], jnp.float32)
    back_rows, gain_one_term = norm_back(grad_normed, rows, scale_one, gain_a)
    grad_rows = (grad_mid + back_rows).astype(half_type).reshape(batch, group, width)
    gain_terms = jnp.stack([gain_one_term, gain_two_term])
    one_a.receive(flow.round([one_a.move()])[0])
    bits = [0] + list(upper)
    for step in range(len(upper)):
        send(one)
        got = exchange(one, [(gain_terms, bits.pop(0))])
        gain_terms = gain_terms + got[0]
    done = [job.line() for job in one]
    one_done = finish(one)
    first_done, out_done = one_done[:, : one_done.shape[1] - width], one_done[:, -width:]
    for bit in bits:
        gain_terms = gain_terms + partner(gain_terms, bit)
    gain_terms = sum(
        [around(gain_terms, steps) for steps in range(1, lax.axis_size("seq"))], gain_terms
    )
    owned = gain_one.shape[0]
    mine = (lax.axis_index("dp") * lax.axis_size("seq") + lax.axis_index("seq")) * owned
    gain_done = lax.dynamic_slice_in_dim(gain_terms, mine, owned, 1)
    return (
        output,
        grad_rows,
        gain_done[0],
        first_done[:, :inner],
        first_done[:, inner : inner + HEAD],
        first_done[:, inner + HEAD :],
        out_done,
        gain_done[1],
        gate_done,
        up_done,
        down_done,
    )


def solution(mesh):
    in_specs = (
        P("dp", "seq", None),
        P("dp", None),
        P(("dp", "seq")),
        P(("dp", "seq"), None),
        P(("dp", "seq"), None),
        P(("dp", "seq"), None),
        P(("dp", "seq"), None),
        P(("dp", "seq")),
        P(("dp", "seq"), None),
        P(("dp", "seq"), None),
        P(("dp", "seq"), None),
        P("dp", "seq", None),
    )
    out_specs = (
        P("dp", "seq", None),
        P("dp", "seq", None),
        P(("dp", "seq")),
        P(("dp", "seq"), None),
        P(("dp", "seq"), None),
        P(("dp", "seq"), None),
        P(("dp", "seq"), None),
        P(("dp", "seq")),
        P(("dp", "seq"), None),
        P(("dp", "seq"), None),
        P(("dp", "seq"), None),
    )
    return jax.shard_map(
        on_device, mesh=mesh, in_specs=in_specs, out_specs=out_specs, check_vma=False
    )
```

```python
import functools
import math

import jax
import jax.numpy as jnp
from jax import lax
from jax.experimental import pallas as pl
from jax.experimental.pallas import tpu as pltpu
from jax.sharding import PartitionSpec as P

HEADS = 16
HEAD = 128
WINDOW = 512


EPS = 1e-05


def shifted(value, axis, steps):
    count = lax.axis_size(axis)
    initial, last = (max(0, -steps), min(count, count - steps))
    return lax.ppermute(value, axis, [(source, source + steps) for source in range(initial, last)])


def documents(doc_lengths, index):
    ends = jnp.cumsum(doc_lengths, axis=-1)
    passed = (index[None, :, None] >= ends[:, None, :]).astype(jnp.int32)
    segment = jnp.sum(passed, axis=-1)
    before = jnp.sum(passed * doc_lengths[:, None, :], axis=-1)
    return (segment, index[None, :] - before)


def rope_tables(position):
    half = HEAD // 2
    freq = jnp.exp(jnp.arange(half, dtype=jnp.float32) * (-2.0 * math.log(10000.0) / HEAD))
    angles = position.astype(jnp.float32)[..., None] * freq
    return (jnp.cos(angles), jnp.sin(angles))


def rotate(vec, cosine, sine):
    half = vec.shape[-1] // 2
    first = vec[..., :half]
    second = vec[..., half:]
    return jnp.concatenate(
        [first * cosine - second * sine, second * cosine + first * sine], axis=-1
    )


def norm_back(grad_normed, rows, scale, gain):
    inner = grad_normed * gain
    grad_gain = jnp.sum(grad_normed * rows * scale, axis=0)
    grad_rows = scale * inner - rows * (scale * scale * scale) * jnp.mean(
        inner * rows, axis=-1, keepdims=True
    )
    return (grad_rows, grad_gain)


def matmul(left, right):
    return jnp.dot(left, right, preferred_element_type=jnp.float32)


def after(values, *others):
    return lax.optimization_barrier((values, others))[0]


def partner(value, bit):
    count = lax.axis_size("dp")
    return lax.ppermute(value, "dp", [(source, source ^ (1 << bit)) for source in range(count)])


def around(value, steps):
    count = lax.axis_size("seq")
    return lax.ppermute(
        value, "seq", [(source, (source + steps) % count) for source in range(count)]
    )


def dp_bits():
    return lax.axis_size("dp").bit_length() - 1


MIB = 1 << 20
ANYWHERE = pl.BlockSpec(memory_space=pl.ANY)


def kernel_params(flops, traffic):
    return {
        "compiler_params": pltpu.CompilerParams(vmem_limit_bytes=58 * MIB),
        "cost_estimate": pl.CostEstimate(
            flops=flops, bytes_accessed=traffic, transcendentals=0
        ),
    }


def owner(number):
    return lax.bitwise_xor(lax.axis_index("dp"), number)


def rows_kernel(count, gained, near, left, *refs):
    pieces, rest = refs[:count], refs[count:]
    if gained:
        out, normed, gains, held, sems = rest
    else:
        out, held, sems = rest
    step = pl.program_id(0)
    rows, columns = held.shape[1], out.shape[1]
    copies = [
        pltpu.make_async_copy(piece, held.at[number], sems.at[number])
        for number, piece in enumerate(pieces)
    ]

    @pl.when(step == 0)
    def _():
        for copy in copies:
            copy.start()

    for number, copy in enumerate(copies):

        @pl.when(step == number)
        def _(copy=copy):
            copy.wait()

    start = pl.multiple_of(owner(step) * rows, rows)
    block = left[:, pl.ds(start, rows)]
    if gained:
        turned = held[step, :, columns:].astype(jnp.float32).T
        gains[...] = turned[:8]
        block = (block * turned[:1]).astype(normed.dtype)
        normed[...] = block
    part = matmul(block, held[step, :, :columns])

    @pl.when(step == 0)
    def _():
        out[...] = part

    @pl.when(step > 0)
    def _():
        out[...] += part


def near_places(count):
    return lax.bitwise_xor(lax.axis_index("dp"), jnp.arange(count, dtype=jnp.int32))


def by_rows(left, held, columns):
    count, (rows, wide) = len(held), held[0].shape
    tokens = left.shape[0]
    gained = wide > columns
    out_shape = [jax.ShapeDtypeStruct((tokens, columns), jnp.float32)]
    out_specs = [pl.BlockSpec((tokens, columns), lambda step, near: (0, 0))]
    if gained:
        out_shape += [
            jax.ShapeDtypeStruct(left.shape, held[0].dtype),
            jax.ShapeDtypeStruct((8, left.shape[1]), jnp.float32),
        ]
        out_specs += [
            pl.BlockSpec((tokens, rows), lambda step, near: (0, near[step])),
            pl.BlockSpec((8, rows), lambda step, near: (0, near[step])),
        ]
    return pl.pallas_call(
        functools.partial(rows_kernel, count, gained),
        out_shape=out_shape,
        grid_spec=pltpu.PrefetchScalarGridSpec(
            num_scalar_prefetch=1,
            grid=(count,),
            in_specs=[pl.BlockSpec(left.shape, lambda step, near: (0, 0))] + [ANYWHERE] * count,
            out_specs=out_specs,
            scratch_shapes=[
                pltpu.VMEM((count, rows, wide), held[0].dtype),
                pltpu.SemaphoreType.DMA((count,)),
            ],
        ),
        **kernel_params(2 * tokens * count * rows * columns, 2 * count * rows * columns),
    )(near_places(count), left, *[held[place] for place in range(count)])


def back_kernel(count, many, near, *refs):
    lefts = refs[:many]
    pieces = refs[many : many + many * count]
    out, held, sems = refs[many + many * count :]
    step = pl.program_id(0)

    def copy(number, which, slot):
        return pltpu.make_async_copy(
            pieces[which * count + number], held.at[slot, which], sems.at[slot, which]
        )

    for number in range(count):

        @pl.when(step == max(number - 1, 0))
        def _(number=number):
            for which in range(many):
                copy(number, which, number % 2).start()

    slot = lax.rem(step, 2)
    total = None
    for which in range(many):
        copy(0, which, slot).wait()
        part = lax.dot_general(
            lefts[which][...],
            held[slot, which, :, : lefts[which].shape[1]],
            (((1,), (1,)), ((), ())),
            preferred_element_type=jnp.float32,
        )
        total = part if total is None else total + part
    out[...] = total.astype(out.dtype)


def back_by_rows(lefts, helds, dtype):
    count, many = len(helds[0]), len(lefts)
    rows, wide = helds[0][0].shape
    tokens, columns = lefts[0].shape
    near = near_places(count)
    return pl.pallas_call(
        functools.partial(back_kernel, count, many),
        out_shape=jax.ShapeDtypeStruct((tokens, count * rows), dtype),
        grid_spec=pltpu.PrefetchScalarGridSpec(
            num_scalar_prefetch=1,
            grid=(count,),
            in_specs=[pl.BlockSpec((tokens, columns), lambda step, near: (0, 0))] * many
            + [ANYWHERE] * (many * count),
            out_specs=pl.BlockSpec((tokens, rows), lambda step, near: (0, near[step])),
            scratch_shapes=[
                pltpu.VMEM((2, many, rows, wide), helds[0][0].dtype),
                pltpu.SemaphoreType.DMA((2, many)),
            ],
        ),
        **kernel_params(
            2 * tokens * many * count * rows * columns, 2 * many * count * rows * columns
        ),
    )(near, *lefts, *[held[place] for held in helds for place in range(count)])


def across_rows(left, right):
    return lax.dot_general(
        left, right, (((1,), (1,)), ((), ())), preferred_element_type=jnp.float32
    )


def attend_kernel(bias, query, keys, values_turned, mixed, log_total):
    block = min(256, query.shape[0])
    for number in range(query.shape[0] // block):
        mine = slice(number * block, (number + 1) * block)
        seen = slice(number * block, (number + 1) * block + WINDOW)
        scores = across_rows(keys[seen, :], query[mine, :]) * (1.0 / math.sqrt(HEAD))
        scores = scores + bias[seen, mine]
        top = jnp.max(scores, axis=0, keepdims=True)
        weight = jnp.exp(scores - top)
        total = jnp.sum(weight, axis=0, keepdims=True)
        probs = (weight * (1.0 / total)).astype(jnp.bfloat16)
        mixed[mine, :] = matmul(values_turned[:, seen], probs).T.astype(mixed.dtype)
        log_total[0, :, mine] = top + jnp.log(total)


def head_specs(group, length):
    def whole(*shape):
        return pl.BlockSpec(shape, lambda head: (0, 0))

    column = pl.BlockSpec((group, HEAD), lambda head: (0, head))
    row = pl.BlockSpec((1, 1, group), lambda head: (head, 0, 0))
    return whole, column, row


def attend(bias, query, keys, values_turned):
    length, group = bias.shape
    whole, column, row = head_specs(group, length)
    heads = query.shape[1] // HEAD
    return pl.pallas_call(
        attend_kernel,
        out_shape=[
            jax.ShapeDtypeStruct(query.shape, query.dtype),
            jax.ShapeDtypeStruct((heads, 1, group), jnp.float32),
        ],
        grid=(heads,),
        in_specs=[whole(length, group), column, whole(length, HEAD), whole(HEAD, length)],
        out_specs=[column, row],
        **kernel_params(4 * length * query.shape[0] * query.shape[1], 8 * query.size),
    )(bias, query, keys, values_turned)


def attend_back_kernel(
    bias, cosine, sine, query, grad_mixed, log_total, keys, keys_turned, values, grad_query,
    grad_keys, grad_values,
):
    block = min(256, query.shape[0])
    factor = 1.0 / math.sqrt(HEAD)

    @pl.when(pl.program_id(0) == 0)
    def _():
        grad_keys[...] = jnp.zeros_like(grad_keys)
        grad_values[...] = jnp.zeros_like(grad_values)

    for number in range(query.shape[0] // block):
        mine = slice(number * block, (number + 1) * block)
        seen = slice(number * block, (number + 1) * block + WINDOW)
        query_rows, grad_rows = query[mine, :], grad_mixed[mine, :]
        scores = across_rows(keys[seen, :], query_rows) * factor + bias[seen, mine]
        probs = jnp.exp(scores - log_total[0, :, mine])
        grad_probs = across_rows(values[seen, :], grad_rows)
        centre = jnp.sum(probs * grad_probs, axis=0, keepdims=True)
        grad_scores = (probs * (grad_probs - centre)).astype(jnp.bfloat16)
        grad_keys[seen, :] += matmul(grad_scores, query_rows) * factor
        grad_values[seen, :] += matmul(probs.astype(jnp.bfloat16), grad_rows)
        turned = matmul(keys_turned[:, seen], grad_scores) * factor
        first, second = turned[: HEAD // 2], turned[HEAD // 2 :]
        cos, sin = cosine[:, mine], sine[:, mine]
        grad_query[mine, :HEAD // 2] = (first * cos + second * sin).T.astype(grad_query.dtype)
        grad_query[mine, HEAD // 2 :] = (second * cos - first * sin).T.astype(grad_query.dtype)


def attend_back(bias, cosine, sine, query, grad_mixed, log_total, keys, values):
    length, group = bias.shape
    whole, column, row = head_specs(group, length)
    heads = query.shape[1] // HEAD
    half = whole(HEAD // 2, group)
    return pl.pallas_call(
        attend_back_kernel,
        out_shape=[
            jax.ShapeDtypeStruct(query.shape, query.dtype),
            jax.ShapeDtypeStruct((length, HEAD), jnp.float32),
            jax.ShapeDtypeStruct((length, HEAD), jnp.float32),
        ],
        grid=(heads,),
        in_specs=[whole(length, group), half, half, column, column, row]
        + [whole(length, HEAD), whole(HEAD, length), whole(length, HEAD)],
        out_specs=[column, whole(length, HEAD), whole(length, HEAD)],
        **kernel_params(10 * length * query.shape[0] * query.shape[1], 12 * query.size),
    )(bias, cosine, sine, query, grad_mixed, log_total, keys, keys.T, values)


def gate_kernel(count, left, *refs):
    pieces = refs[: 2 * count]
    gate, up, hidden, turned, held, sems = refs[2 * count :]
    step, steps = pl.program_id(0), pl.num_programs(0)
    rows, tile = pieces[0].shape[0], gate.shape[1]

    def copies(number, slot):
        column = pl.multiple_of(number * tile, tile)
        for which in range(2):
            for place in range(count):
                start = pl.multiple_of(owner(place) * rows, rows)
                yield pltpu.make_async_copy(
                    pieces[which * count + place].at[:, pl.ds(column, tile)],
                    held.at[slot, which, pl.ds(start, rows), :],
                    sems.at[slot, which, place],
                )

    @pl.when(step == 0)
    def _():
        for copy in copies(0, 0):
            copy.start()

    @pl.when(step + 1 < steps)
    def _():
        for copy in copies(step + 1, lax.rem(step + 1, 2)):
            copy.start()

    slot = lax.rem(step, 2)
    for copy in copies(step, slot):
        copy.wait()
    gate_tile = matmul(left[...], held[slot, 0])
    gate[...] = gate_tile
    up_tile = matmul(left[...], held[slot, 1])
    up[...] = up_tile
    value = (gate_tile * jax.nn.sigmoid(gate_tile) * up_tile).astype(hidden.dtype)
    hidden[...] = value
    turned[...] = value.T


def gate_up(left, gates, ups):
    count, (rows, columns) = len(gates), gates[0].shape
    tokens = left.shape[0]
    tile = next(size for size in (512, 256, 128) if columns % size == 0)
    across = pl.BlockSpec((tokens, tile), lambda step: (0, step))
    return pl.pallas_call(
        functools.partial(gate_kernel, count),
        out_shape=[
            jax.ShapeDtypeStruct((tokens, columns), jnp.float32),
            jax.ShapeDtypeStruct((tokens, columns), jnp.float32),
            jax.ShapeDtypeStruct((tokens, columns), left.dtype),
            jax.ShapeDtypeStruct((columns, tokens), left.dtype),
        ],
        grid=(columns // tile,),
        in_specs=[pl.BlockSpec(left.shape, lambda step: (0, 0))] + [ANYWHERE] * (2 * count),
        out_specs=[across, across, across, pl.BlockSpec((tile, tokens), lambda step: (step, 0))],
        scratch_shapes=[
            pltpu.VMEM((2, 2, count * rows, tile), left.dtype),
            pltpu.SemaphoreType.DMA((2, 2, count)),
        ],
        **kernel_params(
            4 * tokens * count * rows * columns, 4 * columns * (count * rows + 3 * tokens)
        ),
    )(left, *[held[place] for held in (gates, ups) for place in range(count)])


def turn_kernel(source, out):
    out[...] = source[...].T


def turned_over(source):
    rows, columns = source.shape
    return pl.pallas_call(
        turn_kernel,
        out_shape=jax.ShapeDtypeStruct((columns, rows), source.dtype),
        grid=(columns // 512,),
        in_specs=[pl.BlockSpec((rows, 512), lambda step: (0, step))],
        out_specs=pl.BlockSpec((512, rows), lambda step: (step, 0)),
        **kernel_params(0, 4 * rows * columns),
    )(source)


def down_kernel(count, together, sides, back, near, *refs):
    if back:
        gate, up, cot = refs[:3]
        refs = refs[3:]
    else:
        hidden, mid = refs[:2]
        refs = refs[2:]
    own, other = refs[:2]
    halves = len(sides) - 1
    pieces = refs[2 : 2 + halves * count]
    if back:
        grad_gate, grad_up, held, sems = refs[2 + halves * count :]
    else:
        output, held, total, sems = refs[2 + halves * count :]
    step, steps = pl.program_id(0), pl.num_programs(0)
    rows = own.shape[1]

    def copies(number, slot):
        for part in range(together):
            spot = lax.rem(owner(part), together)
            start = pl.multiple_of(spot * rows, rows)
            place = number * together + part
            sources = [(other if place & 1 else own).at[place >> 1]]
            sources += [pieces[half * count + place] for half in range(halves)]
            for which, (left, right) in enumerate(sides):
                yield pltpu.make_async_copy(
                    sources[which],
                    held.at[slot, pl.ds(start, rows), left:right],
                    sems.at[slot, part, which],
                )

    for number in range(count // together):

        @pl.when(step == max(number - 1, 0))
        def _(number=number):
            for copy in copies(number, number % 2):
                copy.start()

    slot = lax.rem(step, 2)
    for copy in copies(0, slot):
        copy.wait()
    weight = held[slot]
    if back:
        grad = across_rows(cot[...], weight)
        gate_rows, up_rows = gate[...], up[...]
        sigma = jax.nn.sigmoid(gate_rows)
        grad_up[...] = (grad * (gate_rows * sigma)).astype(grad_up.dtype)
        grad_gate[...] = (grad * up_rows * (sigma * (1.0 + gate_rows * (1.0 - sigma)))).astype(
            grad_gate.dtype
        )
        return
    added = matmul(hidden[...], weight)

    @pl.when(step == 0)
    def _():
        total[...] = mid[...] + added

    @pl.when(step > 0)
    def _():
        total[...] += added

    @pl.when(step == steps - 1)
    def _():
        output[...] = total[...].astype(output.dtype)


def with_down(operands, early, helds, back):
    count, (blocks, rows, first) = len(helds[0]), early[0].shape
    tokens, width = operands[-1].shape
    ends = [0, first]
    for held in helds:
        ends.append(ends[-1] + held[0].shape[1])
    sides = tuple(zip(ends, ends[1:]))
    together = next(size for size in (2, 4, 8, 16) if size * rows % 128 == 0)
    tile = together * rows
    dp = lax.axis_index("dp")
    near = lax.bitwise_xor(
        lax.div(dp, together), jnp.arange(count // together, dtype=jnp.int32)
    )
    across = pl.BlockSpec((tokens, tile), lambda step, near: (0, near[step]))
    fixed = pl.BlockSpec((tokens, width), lambda step, near: (0, 0))
    columns = count * rows
    wide = jax.ShapeDtypeStruct((tokens, columns), jnp.bfloat16)
    scratch = [pltpu.VMEM((2, tile, width), jnp.bfloat16)]
    if not back:
        scratch.append(pltpu.VMEM((tokens, width), jnp.float32))
    scratch.append(pltpu.SemaphoreType.DMA((2, together, len(sides))))
    return pl.pallas_call(
        functools.partial(down_kernel, count, together, sides, back),
        out_shape=[wide, wide] if back else jax.ShapeDtypeStruct((tokens, width), jnp.bfloat16),
        grid_spec=pltpu.PrefetchScalarGridSpec(
            num_scalar_prefetch=1,
            grid=(count // together,),
            in_specs=([across, across, fixed] if back else [across, fixed])
            + [ANYWHERE] * (2 + len(helds) * count),
            out_specs=[across, across] if back else fixed,
            scratch_shapes=scratch,
        ),
        **kernel_params(2 * tokens * width * columns, 2 * columns * (width + 5 * tokens)),
    )(near, *operands, *early, *[held[place] for held in helds for place in range(count)])


class Flow:
    def __init__(self):
        self.ended = []

    def round(self, moves):
        values = after([value for value, _ in moves], self.ended)
        self.fence = values
        got = [
            bit(value) if callable(bit) else partner(value, bit)
            for value, (_, bit) in zip(values, moves)
        ]
        self.ended = list(got)
        return got

    def holds(self, *results):
        self.ended.extend(results)


def exchange(flow, jobs, also=()):
    moves = [job.moves() for job in jobs]
    got = flow.round([move for found in moves for move in found] + list(also))
    for job, found in zip(jobs, moves):
        job.receive(got[: len(found)])
        got = got[len(found) :]
    return got


class Order:
    def __init__(self):
        self.last = []

    def __call__(self, work, *operands):
        got = work(*after(operands, self.last))
        self.last = [got]
        return got

    def first(self, job):
        job.right = after(job.right, self.last)
        self.last = [job.first()]

    def send(self, job):
        job.right = after(job.right, self.last)
        self.last = list(job.send())

    def line(self, job):
        job.right = after(job.right, self.last)
        self.last = [job.line()]
        return self.last[0]


class Shallow:
    def __init__(self, shard, order):
        self.order, self.pieces, self.level = order, {0: shard}, 0

    def moves(self):
        self.level += 1
        self.places = [
            place
            for place in range(2 << len(self.order))
            if not place & 1 and bin(place).count("1") == self.level
        ]
        found = []
        for place in self.places:
            bit = next(bit for bit in self.order if place >> bit & 1)
            found.append((self.pieces[place ^ (1 << bit)], bit))
        return found

    def put(self, got):
        for place, piece in zip(self.places, got):
            self.pieces[place] = piece

    def left(self):
        return self.level < len(self.order)


class Spreads:
    def __init__(self, order):
        self.order, self.helds = order, [{}, {}]

    def direct(self, flow, number, line, also=()):
        held = self.helds[number]
        held[0] = line
        moves = [(line, 0)] + [(line, bit) for bit in self.order] + list(also)
        got = flow.round(moves)
        held[1] = got[0]
        for bit, piece in zip(self.order, got[1:]):
            held[1 << bit] = piece
        return got[1 + len(self.order) :]

    def both(self, flow, lines):
        got = flow.round([(line, bit) for line in lines for bit in self.order])
        for number, line in enumerate(lines):
            held = self.helds[number]
            held[0] = line
            for place, bit in enumerate(self.order):
                held[1 << bit] = got[number * len(self.order) + place]

    def double(self):
        return [
            (number, place)
            for number, held in enumerate(self.helds)
            for place in sorted(held)
            if not place & 1 and place | 1 not in held
        ]

    def moves(self, names):
        return [(self.helds[number][place], 0) for number, place in names]

    def put(self, names, got):
        for (number, place), piece in zip(names, got):
            self.helds[number][place | 1] = piece

    def cross(self, flow, level, also, cores):
        names, targets, moves = self.double() if cores else [], [], []
        for number, turn in enumerate((self.order, self.order[::-1])):
            for place in range(2 << len(self.order)):
                bits = [bit for bit in turn if place >> bit & 1]
                if not place & 1 and len(bits) == level:
                    targets.append((number, place))
                    moves.append((self.helds[number][place ^ (1 << bits[-1])], bits[-1]))
        got = flow.round(moves + self.moves(names) + list(also))
        for (number, place), piece in zip(targets, got):
            self.helds[number][place] = piece
        end = len(targets) + len(names)
        self.put(names, got[len(targets) : end])
        return got[end:]

    def crosses(self, flow, also=(), cores=True):
        extra = []
        for level in range(2, len(self.order) + 1):
            extra += self.cross(flow, level, also if level == 2 else (), cores)
        return extra


def places_of(order):
    places = [0]
    for bit in reversed(order):
        places = places + [place | (1 << bit) for place in places]
    return places


def sum_kernel(shared, each, table, turned, right, *refs):
    outs = refs[shared + 2 * each :]
    total = matmul(turned[...], right[...])
    for part in refs[:shared]:
        total = total + part[...].astype(jnp.float32)
    sides = 2 if len(outs) == 2 or each else 1
    for side in range(sides):

        @pl.when(pl.program_id(0) == side)
        def _(side=side):
            mine = total
            for part in refs[shared + side * each : shared + (side + 1) * each]:
                mine = mine + part[...].astype(jnp.float32)
            out = outs[side % len(outs)]
            out[...] = mine.astype(out.dtype)


def summed_rows(turned, right, rows, shared=(), parts=((), ()), apart=False):
    sides, count = len(rows), len(rows[0])
    tokens, columns = right.shape[0], right.shape[1] // sides
    block = turned.shape[0] // lax.axis_size("dp")
    table = [[place for side in rows for place in side]]
    table += [[places.index(place) for side in rows for place in side] for _, places in shared]
    for side in range(sides):
        table += [[places.index(place) for place in rows[side]] * sides for _, places in parts[side]]
    spots = jnp.array(table, jnp.int32)
    spots = spots.at[0].set(lax.bitwise_xor(spots[0], lax.axis_index("dp")))
    each = len(parts[0])

    def shared_spec(line):
        return pl.BlockSpec(
            (block, columns),
            lambda now, step, spots: (spots[line, now * count + step], now),
        )

    def one_side(side, row):
        def index(now, step, spots):
            step = jnp.where(now == side, step, jnp.where(now < side, 0, count - 1))
            return (row(step, spots), 0)

        return pl.BlockSpec((block, columns), index)

    def part_spec(side, line):
        return one_side(side, lambda step, spots: spots[line, step])

    if apart:
        out_shape = [jax.ShapeDtypeStruct((count * block, columns), jnp.bfloat16)] * sides
        out_specs = [one_side(side, lambda step, spots: step) for side in range(sides)]
    else:
        out_shape = [jax.ShapeDtypeStruct((count * block, sides * columns), jnp.bfloat16)]
        out_specs = [pl.BlockSpec((block, columns), lambda now, step, spots: (step, now))]
    base = 1 + len(shared)
    return pl.pallas_call(
        functools.partial(sum_kernel, len(shared), each),
        out_shape=out_shape,
        grid_spec=pltpu.PrefetchScalarGridSpec(
            num_scalar_prefetch=1,
            grid=(sides, count),
            in_specs=[
                pl.BlockSpec(
                    (block, tokens),
                    lambda now, step, spots: (spots[0, now * count + step], 0),
                ),
                pl.BlockSpec((tokens, columns), lambda now, step, spots: (0, now)),
            ]
            + [shared_spec(1 + number) for number in range(len(shared))]
            + [
                part_spec(side, base + side * each + number)
                for side in range(sides)
                for number in range(each)
            ],
            out_specs=out_specs,
        ),
        **kernel_params(
            2 * tokens * sides * count * block * columns,
            2 * sides * count * block * columns * (1 + len(shared) + each),
        ),
    )(spots, turned, right, *[part for part, _ in shared], *[p for side in parts for p, _ in side])


class Pair:
    def __init__(self, turned, right, order):
        self.turned, self.right = turned, right
        self.orders = (order, order[::-1])
        self.kept = [places_of(turn) for turn in self.orders]
        self.whole = places_of(order)
        self.shared, self.parts, self.step = [], ([], []), 0

    def first(self):
        places = [place | 1 for place in self.whole]
        self.sent = summed_rows(self.turned, self.right, [places])
        return self.sent[0]

    def first_move(self):
        return (self.sent[0], 0)

    def first_receive(self, got):
        self.shared = [(got, self.whole)]

    def send(self):
        half = len(self.kept[0]) // 2
        self.sent = summed_rows(
            self.turned,
            self.right,
            [kept[half:] for kept in self.kept],
            self.shared,
            self.parts,
            apart=True,
        )
        self.kept = [kept[:half] for kept in self.kept]
        return self.sent

    def moves(self):
        return [(sent, turn[self.step]) for sent, turn in zip(self.sent, self.orders)]

    def receive(self, got):
        for piece, parts, kept in zip(got, self.parts, self.kept):
            parts.append((piece, kept))
        self.step += 1

    def left(self):
        return len(self.orders[0]) - self.step

    def line(self):
        self.sent = summed_rows(self.turned, self.right, self.kept, self.shared, self.parts)
        return self.sent[0]


def finish(line):
    return lax.psum_scatter(line, "seq", scatter_dimension=0, tiled=True).astype(jnp.float32)


class Halved:
    def __init__(self, blocks, order):
        self.order, self.step = order, 0
        self.kept = [block.astype(jnp.float32) for block in blocks]

    def left(self):
        return len(self.order) - self.step

    def moves(self):
        half = len(self.kept) // 2
        sent = jnp.concatenate(self.kept[half:], axis=0).astype(jnp.bfloat16)
        self.kept = self.kept[:half]
        return [(sent, self.order[self.step])]

    def receive(self, got):
        (got,) = got
        rows = got.shape[0] // len(self.kept)
        self.kept = [
            kept + got[number * rows : (number + 1) * rows].astype(jnp.float32)
            for number, kept in enumerate(self.kept)
        ]
        self.step += 1


def on_device(
    tokens,
    lengths,
    gain_one,
    w_query,
    w_key,
    w_value,
    w_out,
    gain_two,
    w_gate,
    w_up,
    w_down,
    cotangent,
):
    half_type = jnp.bfloat16
    batch, group, width = tokens.shape
    count = batch * group
    upper = tuple(range(1, dp_bits()))
    inner = w_query.shape[1]
    middle = w_down.shape[1] // 2

    def along(shard):
        return lax.all_gather(shard, "seq", axis=0, tiled=True)

    gains = jnp.stack([gain_one, gain_two], axis=1)
    first = jnp.concatenate(
        [w_query, w_key, w_value, jnp.pad(gains, ((0, 0), (0, HEAD - 2)))], axis=1
    ).astype(half_type)
    columns_first = inner + 2 * HEAD
    flow = Flow()
    line_first = along(first)
    line_out = along(after(w_out.astype(half_type), line_first))
    one_spread, two_spread, three_spread = Spreads(upper), Spreads(upper), Spreads(upper)
    one_spread.direct(flow, 0, line_first)
    line_gate = along(after(w_gate.astype(half_type), line_out, flow.ended))
    line_up = along(after(w_up.astype(half_type), line_gate))
    down_half = w_down.astype(half_type)
    quarter = middle + middle // 2
    line_right = along(after(down_half[:, middle:], line_up))
    early_spread = Shallow(down_half[:, :middle], upper)
    flow.holds(line_out)
    early_spread.put(one_spread.direct(flow, 1, line_out, early_spread.moves()))
    one_spread.crosses(flow)
    flow.holds(line_gate)
    left_over = one_spread.double()
    one_spread.put(
        left_over, two_spread.direct(flow, 0, line_gate, one_spread.moves(left_over))
    )
    full_one = one_spread.helds

    reach = (WINDOW - 2) // group + 1
    offset = lax.axis_index("seq") * group
    query_at = offset + jnp.arange(group, dtype=jnp.int32)
    key_at = offset - reach * group + jnp.arange((reach + 1) * group, dtype=jnp.int32)
    query_seg, query_pos = documents(lengths, query_at)
    key_seg = documents(lengths, key_at)[0]
    allowed = (
        (key_at[None, :] >= 0)
        & (query_at[:, None] >= key_at[None, :])
        & (query_at[:, None] - key_at[None, :] < WINDOW)
    )
    allowed = allowed & (query_seg[0][:, None] == key_seg[0][None, :])
    bias = jnp.where(allowed.T, 0.0, -1e30)
    cosine, sine = rope_tables(query_pos)
    rows = tokens.astype(jnp.float32).reshape(count, width)
    scale_one = lax.rsqrt(jnp.mean(rows * rows, axis=-1, keepdims=True) + EPS)
    mapped, normed, gain_rows = by_rows(rows * scale_one, full_one[0], columns_first)
    gain_a, gain_b = gain_rows[0], gain_rows[1]
    query = mapped[:, :inner].reshape(batch, group, HEADS, HEAD)
    key = mapped[:, inner : inner + HEAD].reshape(batch, group, HEAD)
    value = mapped[:, inner + HEAD :].astype(half_type).reshape(batch, group, HEAD)
    query_turned = rotate(query, cosine[:, :, None, :], sine[:, :, None, :]).astype(half_type)
    key_turned = rotate(key, cosine, sine).astype(half_type)
    paired = jnp.concatenate([key_turned, value], axis=-1)
    pieces = []
    for step in range(reach, 0, -1):
        pieces.append(shifted(paired, "seq", step))
    pieces.append(paired)
    seen = jnp.concatenate(pieces, axis=1)
    keys_seen = seen[..., :HEAD]
    values_seen = seen[..., HEAD:]

    query_turned = query_turned.reshape(count, HEADS * HEAD)
    keys_seen, values_seen = keys_seen[0], values_seen[0]
    flow.holds(line_up, query_turned)
    early_spread.put(two_spread.direct(flow, 1, line_up, early_spread.moves()))
    while early_spread.left():
        early_spread.put(flow.round(early_spread.moves()))
    places = sorted(early_spread.pieces)
    early = jnp.stack([early_spread.pieces[place] for place in places])
    early = lax.all_gather(after(early, line_right), "seq", axis=1, tiled=True)
    mixed, log_total = attend(bias, query_turned, keys_seen, values_seen.T)
    mid = rows + by_rows(mixed, full_one[1], width)[0]
    scale_two = lax.rsqrt(jnp.mean(mid * mid, axis=-1, keepdims=True) + EPS)
    normed_two = (mid * scale_two * gain_b).astype(half_type)

    turned_one, turned_mixed, turned_two = map(turned_over, (normed, mixed, normed_two))
    flow.holds(normed_two, line_right, turned_one, turned_mixed, turned_two)
    two_spread.crosses(flow)
    left_over = two_spread.double()
    lines_three = [line_right[:, : quarter - middle], line_right[:, quarter - middle :]]
    got = flow.round(two_spread.moves(left_over) + [(line, 0) for line in lines_three])
    two_spread.put(left_over, got)
    for held, piece in zip(three_spread.helds, got[len(left_over) :]):
        held[1] = piece
    full_two = two_spread.helds
    three_spread.both(flow, lines_three)
    order = Order()
    gate, up_val, hidden, hidden_turned = order(
        lambda left: gate_up(left, *full_two), normed_two
    )

    grad_out = cotangent.reshape(count, width)
    flow.holds(order.last)
    early = [early] + three_spread.crosses(flow, [(early, 0)], False)
    job_down = Pair(hidden_turned, grad_out, upper)
    order.first(job_down)
    flow.holds(order.last)
    left_over = three_spread.double()
    three_spread.put(left_over, flow.round(three_spread.moves(left_over)))
    job_down.first_receive(partner(after(job_down.sent[0], flow.ended), 0))
    full_three = three_spread.helds
    grad_gate, grad_up = order(
        lambda *operands: with_down(operands, early, full_three, True), gate, up_val, grad_out
    )
    job_gate = Pair(turned_two, grad_gate, upper)
    job_up = Pair(turned_two, grad_up, upper)

    def rest(job):
        while job.left() > 1:
            order.send(job)
            exchange(flow, [job])

    order.first(job_gate)
    job_gate.first_receive(partner(*job_gate.first_move()))
    order.first(job_up)
    job_down.right = after(job_down.right, order.last)
    order.last = summed_rows(job_down.turned, job_down.right, [job_down.whole], job_down.shared)
    down_parts = lax.psum_scatter(
        order.last[0].reshape(len(places), -1, width), "seq", scatter_dimension=1, tiled=True
    )
    sums = []
    for turn, part in (
        (upper, down_parts[:, :, :middle]),
        (upper[::-1], down_parts[:, :, middle:]),
    ):
        sums.append(Halved([part[job_down.whole.index(place)] for place in places_of(turn)], turn))
    order.send(job_gate)
    flow.holds(order.last)
    job_up.first_receive(exchange(flow, [job_gate], [job_up.first_move()])[0])

    grad_normed_two = order(
        lambda *lefts: back_by_rows(lefts, full_two, jnp.float32), grad_gate, grad_up
    )
    back_mid, gain_two_term = norm_back(grad_normed_two, mid, scale_two, gain_b)
    grad_mid = grad_out.astype(jnp.float32) + back_mid
    grad_branch = grad_mid.astype(half_type)
    job_out = Pair(turned_mixed, grad_branch, upper)
    order.last = [grad_branch]
    order.first(job_out)
    order.send(job_up)
    flow.holds(order.last)
    job_out.first_receive(exchange(flow, [job_up], [job_out.first_move()])[0])

    rest(job_gate)
    order.send(job_gate)
    grad_mixed = order(lambda left: back_by_rows([left], full_one[1:], half_type), grad_branch)
    grad_q, grad_keys, grad_values = order(
        lambda left: attend_back(
            bias, cosine[0].T, sine[0].T, query_turned, left, log_total, keys_seen, values_seen
        ),
        grad_mixed,
    )
    flow.holds(order.last)
    exchange(flow, [job_gate])

    grad_seen = jnp.concatenate([grad_keys, grad_values], axis=-1)[None]
    own, arrived = grad_seen[:, reach * group :], []
    for step in range(1, reach + 1):
        part = grad_seen[:, (reach - step) * group : (reach - step + 1) * group]
        part = shifted(part.astype(jnp.bfloat16), "seq", -step)
        arrived.append(part)
        own = own + part.astype(own.dtype)
    grad_key = rotate(own[..., :HEAD], cosine, -sine).astype(half_type).reshape(count, HEAD)
    grad_value = own[..., HEAD:].astype(half_type).reshape(count, HEAD)
    rest(job_up)
    order.send(job_up)
    output = order(
        lambda *operands: with_down(operands, early, full_three, False), hidden, mid
    ).reshape(batch, group, width)
    flow.holds(order.last)
    exchange(flow, [job_up])

    gate_done = finish(order.line(job_gate))
    order.send(job_out)
    flow.holds(order.last, down_parts, arrived)
    exchange(flow, [job_out])

    grad_first = jnp.concatenate([grad_q, grad_key, grad_value], axis=1)
    job_first = Pair(turned_one, after(grad_first, flow.fence), upper)
    order.first(job_first)
    job_first.first_receive(partner(*job_first.first_move()))
    up_done = finish(order.line(job_up))
    flow.holds(order.last)
    exchange(flow, sums)

    order.send(job_first)
    flow.holds(order.last)
    exchange(flow, [job_first])

    rest(job_out)
    order.send(job_out)
    grad_normed = order(
        lambda left: back_by_rows([left], full_one[:1], jnp.float32), grad_first
    )
    flow.holds(order.last)
    exchange(flow, [job_out])

    rest(job_first)
    order.send(job_first)
    flow.holds(order.last)
    exchange(flow, [job_first])
    back_rows, gain_one_term = norm_back(grad_normed, rows, scale_one, gain_a)
    grad_rows = (grad_mid + back_rows).astype(half_type).reshape(batch, group, width)
    gain_terms = jnp.stack([gain_one_term, gain_two_term])

    out_done = finish(order.line(job_out))
    first_done = finish(order.line(job_first))
    while sums[0].left():
        exchange(flow, sums)
    down_done = jnp.concatenate([part.kept[0] for part in sums], axis=1)
    bits = range(dp_bits())
    for bit in bits:
        gain_terms = gain_terms + partner(gain_terms, bit)
    gain_terms = sum(
        [around(gain_terms, steps) for steps in range(1, lax.axis_size("seq"))], gain_terms
    )
    owned = gain_one.shape[0]
    mine = (lax.axis_index("dp") * lax.axis_size("seq") + lax.axis_index("seq")) * owned
    gain_done = lax.dynamic_slice_in_dim(gain_terms, mine, owned, 1)
    return (
        output,
        grad_rows,
        gain_done[0],
        first_done[:, :inner],
        first_done[:, inner : inner + HEAD],
        first_done[:, inner + HEAD :],
        out_done,
        gain_done[1],
        gate_done,
        up_done,
        down_done,
    )


def solution(mesh):
    in_specs = (
        P("dp", "seq", None),
        P("dp", None),
        P(("dp", "seq")),
        P(("dp", "seq"), None),
        P(("dp", "seq"), None),
        P(("dp", "seq"), None),
        P(("dp", "seq"), None),
        P(("dp", "seq")),
        P(("dp", "seq"), None),
        P(("dp", "seq"), None),
        P(("dp", "seq"), None),
        P("dp", "seq", None),
    )
    out_specs = (
        P("dp", "seq", None),
        P("dp", "seq", None),
        P(("dp", "seq")),
        P(("dp", "seq"), None),
        P(("dp", "seq"), None),
        P(("dp", "seq"), None),
        P(("dp", "seq"), None),
        P(("dp", "seq")),
        P(("dp", "seq"), None),
        P(("dp", "seq"), None),
        P(("dp", "seq"), None),
    )
    return jax.shard_map(
        on_device, mesh=mesh, in_specs=in_specs, out_specs=out_specs, check_vma=False
    )
```

```python
import functools
import math

import jax
import jax.numpy as jnp
from jax import lax
from jax.experimental import pallas as pl
from jax.experimental.pallas import tpu as pltpu
from jax.sharding import PartitionSpec as P

HEADS = 16
HEAD = 128
WINDOW = 512


EPS = 1e-05


def shifted(value, axis, steps):
    count = lax.axis_size(axis)
    initial, last = (max(0, -steps), min(count, count - steps))
    return lax.ppermute(value, axis, [(source, source + steps) for source in range(initial, last)])


def documents(doc_lengths, index):
    ends = jnp.cumsum(doc_lengths, axis=-1)
    passed = (index[None, :, None] >= ends[:, None, :]).astype(jnp.int32)
    segment = jnp.sum(passed, axis=-1)
    before = jnp.sum(passed * doc_lengths[:, None, :], axis=-1)
    return (segment, index[None, :] - before)


def rope_tables(position):
    half = HEAD // 2
    freq = jnp.exp(jnp.arange(half, dtype=jnp.float32) * (-2.0 * math.log(10000.0) / HEAD))
    angles = position.astype(jnp.float32)[..., None] * freq
    return (jnp.cos(angles), jnp.sin(angles))


def rotate(vec, cosine, sine):
    half = vec.shape[-1] // 2
    first = vec[..., :half]
    second = vec[..., half:]
    return jnp.concatenate(
        [first * cosine - second * sine, second * cosine + first * sine], axis=-1
    )


def norm_back(grad_normed, rows, scale, gain):
    inner = grad_normed * gain
    grad_gain = jnp.sum(grad_normed * rows * scale, axis=0)
    grad_rows = scale * inner - rows * (scale * scale * scale) * jnp.mean(
        inner * rows, axis=-1, keepdims=True
    )
    return (grad_rows, grad_gain)


def matmul(left, right):
    return jnp.dot(left, right, preferred_element_type=jnp.float32)


def after(values, *others):
    return lax.optimization_barrier((values, others))[0]


def partner(value, bit):
    count = lax.axis_size("dp")
    return lax.ppermute(value, "dp", [(source, source ^ (1 << bit)) for source in range(count)])


def around(value, steps):
    count = lax.axis_size("seq")
    return lax.ppermute(
        value, "seq", [(source, (source + steps) % count) for source in range(count)]
    )


def dp_bits():
    return lax.axis_size("dp").bit_length() - 1


MIB = 1 << 20
ANYWHERE = pl.BlockSpec(memory_space=pl.ANY)


def kernel_params(flops, traffic):
    return {
        "compiler_params": pltpu.CompilerParams(vmem_limit_bytes=58 * MIB),
        "cost_estimate": pl.CostEstimate(
            flops=flops, bytes_accessed=traffic, transcendentals=0
        ),
    }


def owner(number):
    return lax.bitwise_xor(lax.axis_index("dp"), number)


def rows_kernel(count, gained, near, left, *refs):
    pieces, rest = refs[:count], refs[count:]
    if gained:
        out, normed, gains, held, sems = rest
    else:
        out, held, sems = rest
    step = pl.program_id(0)
    rows, columns = held.shape[1], out.shape[1]
    copies = [
        pltpu.make_async_copy(piece, held.at[number], sems.at[number])
        for number, piece in enumerate(pieces)
    ]

    @pl.when(step == 0)
    def _():
        for copy in copies:
            copy.start()

    for number, copy in enumerate(copies):

        @pl.when(step == number)
        def _(copy=copy):
            copy.wait()

    start = pl.multiple_of(owner(step) * rows, rows)
    block = left[:, pl.ds(start, rows)]
    if gained:
        turned = held[step, :, columns:].astype(jnp.float32).T
        gains[...] = turned[:8]
        block = (block * turned[:1]).astype(normed.dtype)
        normed[...] = block
    part = matmul(block, held[step, :, :columns])

    @pl.when(step == 0)
    def _():
        out[...] = part

    @pl.when(step > 0)
    def _():
        out[...] += part


def near_places(count):
    return lax.bitwise_xor(lax.axis_index("dp"), jnp.arange(count, dtype=jnp.int32))


def by_rows(left, held, columns):
    count, (rows, wide) = len(held), held[0].shape
    tokens = left.shape[0]
    gained = wide > columns
    out_shape = [jax.ShapeDtypeStruct((tokens, columns), jnp.float32)]
    out_specs = [pl.BlockSpec((tokens, columns), lambda step, near: (0, 0))]
    if gained:
        out_shape += [
            jax.ShapeDtypeStruct(left.shape, held[0].dtype),
            jax.ShapeDtypeStruct((8, left.shape[1]), jnp.float32),
        ]
        out_specs += [
            pl.BlockSpec((tokens, rows), lambda step, near: (0, near[step])),
            pl.BlockSpec((8, rows), lambda step, near: (0, near[step])),
        ]
    return pl.pallas_call(
        functools.partial(rows_kernel, count, gained),
        out_shape=out_shape,
        grid_spec=pltpu.PrefetchScalarGridSpec(
            num_scalar_prefetch=1,
            grid=(count,),
            in_specs=[pl.BlockSpec(left.shape, lambda step, near: (0, 0))] + [ANYWHERE] * count,
            out_specs=out_specs,
            scratch_shapes=[
                pltpu.VMEM((count, rows, wide), held[0].dtype),
                pltpu.SemaphoreType.DMA((count,)),
            ],
        ),
        **kernel_params(2 * tokens * count * rows * columns, 2 * count * rows * columns),
    )(near_places(count), left, *[held[place] for place in range(count)])


def back_kernel(count, many, near, *refs):
    lefts = refs[:many]
    pieces = refs[many : many + many * count]
    out, held, sems = refs[many + many * count :]
    step = pl.program_id(0)

    def copy(number, which, slot):
        return pltpu.make_async_copy(
            pieces[which * count + number], held.at[slot, which], sems.at[slot, which]
        )

    for number in range(count):

        @pl.when(step == max(number - 1, 0))
        def _(number=number):
            for which in range(many):
                copy(number, which, number % 2).start()

    slot = lax.rem(step, 2)
    total = None
    for which in range(many):
        copy(0, which, slot).wait()
        part = lax.dot_general(
            lefts[which][...],
            held[slot, which, :, : lefts[which].shape[1]],
            (((1,), (1,)), ((), ())),
            preferred_element_type=jnp.float32,
        )
        total = part if total is None else total + part
    out[...] = total.astype(out.dtype)


def back_by_rows(lefts, helds, dtype):
    count, many = len(helds[0]), len(lefts)
    rows, wide = helds[0][0].shape
    tokens, columns = lefts[0].shape
    near = near_places(count)
    return pl.pallas_call(
        functools.partial(back_kernel, count, many),
        out_shape=jax.ShapeDtypeStruct((tokens, count * rows), dtype),
        grid_spec=pltpu.PrefetchScalarGridSpec(
            num_scalar_prefetch=1,
            grid=(count,),
            in_specs=[pl.BlockSpec((tokens, columns), lambda step, near: (0, 0))] * many
            + [ANYWHERE] * (many * count),
            out_specs=pl.BlockSpec((tokens, rows), lambda step, near: (0, near[step])),
            scratch_shapes=[
                pltpu.VMEM((2, many, rows, wide), helds[0][0].dtype),
                pltpu.SemaphoreType.DMA((2, many)),
            ],
        ),
        **kernel_params(
            2 * tokens * many * count * rows * columns, 2 * many * count * rows * columns
        ),
    )(near, *lefts, *[held[place] for held in helds for place in range(count)])


def across_rows(left, right):
    return lax.dot_general(
        left, right, (((1,), (1,)), ((), ())), preferred_element_type=jnp.float32
    )


def attend_kernel(bias, query, keys, values_turned, mixed, log_total):
    block = min(256, query.shape[0])
    for number in range(query.shape[0] // block):
        mine = slice(number * block, (number + 1) * block)
        seen = slice(number * block, (number + 1) * block + WINDOW)
        scores = across_rows(keys[seen, :], query[mine, :]) * (1.0 / math.sqrt(HEAD))
        scores = scores + bias[seen, mine]
        top = jnp.max(scores, axis=0, keepdims=True)
        weight = jnp.exp(scores - top)
        total = jnp.sum(weight, axis=0, keepdims=True)
        probs = (weight * (1.0 / total)).astype(jnp.bfloat16)
        mixed[mine, :] = matmul(values_turned[:, seen], probs).T.astype(mixed.dtype)
        log_total[0, :, mine] = top + jnp.log(total)


def head_specs(group, length):
    def whole(*shape):
        return pl.BlockSpec(shape, lambda head: (0, 0))

    column = pl.BlockSpec((group, HEAD), lambda head: (0, head))
    row = pl.BlockSpec((1, 1, group), lambda head: (head, 0, 0))
    return whole, column, row


def attend(bias, query, keys, values_turned):
    length, group = bias.shape
    whole, column, row = head_specs(group, length)
    heads = query.shape[1] // HEAD
    return pl.pallas_call(
        attend_kernel,
        out_shape=[
            jax.ShapeDtypeStruct(query.shape, query.dtype),
            jax.ShapeDtypeStruct((heads, 1, group), jnp.float32),
        ],
        grid=(heads,),
        in_specs=[whole(length, group), column, whole(length, HEAD), whole(HEAD, length)],
        out_specs=[column, row],
        **kernel_params(4 * length * query.shape[0] * query.shape[1], 8 * query.size),
    )(bias, query, keys, values_turned)


def attend_back_kernel(
    bias, cosine, sine, query, grad_mixed, log_total, keys, keys_turned, values, grad_query,
    grad_keys, grad_values,
):
    block = min(256, query.shape[0])
    factor = 1.0 / math.sqrt(HEAD)

    @pl.when(pl.program_id(0) == 0)
    def _():
        grad_keys[...] = jnp.zeros_like(grad_keys)
        grad_values[...] = jnp.zeros_like(grad_values)

    for number in range(query.shape[0] // block):
        mine = slice(number * block, (number + 1) * block)
        seen = slice(number * block, (number + 1) * block + WINDOW)
        query_rows, grad_rows = query[mine, :], grad_mixed[mine, :]
        scores = across_rows(keys[seen, :], query_rows) * factor + bias[seen, mine]
        probs = jnp.exp(scores - log_total[0, :, mine])
        grad_probs = across_rows(values[seen, :], grad_rows)
        centre = jnp.sum(probs * grad_probs, axis=0, keepdims=True)
        grad_scores = (probs * (grad_probs - centre)).astype(jnp.bfloat16)
        grad_keys[seen, :] += matmul(grad_scores, query_rows) * factor
        grad_values[seen, :] += matmul(probs.astype(jnp.bfloat16), grad_rows)
        turned = matmul(keys_turned[:, seen], grad_scores) * factor
        first, second = turned[: HEAD // 2], turned[HEAD // 2 :]
        cos, sin = cosine[:, mine], sine[:, mine]
        grad_query[mine, :HEAD // 2] = (first * cos + second * sin).T.astype(grad_query.dtype)
        grad_query[mine, HEAD // 2 :] = (second * cos - first * sin).T.astype(grad_query.dtype)


def attend_back(bias, cosine, sine, query, grad_mixed, log_total, keys, values):
    length, group = bias.shape
    whole, column, row = head_specs(group, length)
    heads = query.shape[1] // HEAD
    half = whole(HEAD // 2, group)
    return pl.pallas_call(
        attend_back_kernel,
        out_shape=[
            jax.ShapeDtypeStruct(query.shape, query.dtype),
            jax.ShapeDtypeStruct((length, HEAD), jnp.float32),
            jax.ShapeDtypeStruct((length, HEAD), jnp.float32),
        ],
        grid=(heads,),
        in_specs=[whole(length, group), half, half, column, column, row]
        + [whole(length, HEAD), whole(HEAD, length), whole(length, HEAD)],
        out_specs=[column, whole(length, HEAD), whole(length, HEAD)],
        **kernel_params(10 * length * query.shape[0] * query.shape[1], 12 * query.size),
    )(bias, cosine, sine, query, grad_mixed, log_total, keys, keys.T, values)


def gate_kernel(count, left, *refs):
    pieces = refs[: 2 * count]
    gate, up, hidden, turned, held, sems = refs[2 * count :]
    step, steps = pl.program_id(0), pl.num_programs(0)
    rows, tile = pieces[0].shape[0], gate.shape[1]

    def copies(number, slot):
        column = pl.multiple_of(number * tile, tile)
        for which in range(2):
            for place in range(count):
                start = pl.multiple_of(owner(place) * rows, rows)
                yield pltpu.make_async_copy(
                    pieces[which * count + place].at[:, pl.ds(column, tile)],
                    held.at[slot, which, pl.ds(start, rows), :],
                    sems.at[slot, which, place],
                )

    @pl.when(step == 0)
    def _():
        for copy in copies(0, 0):
            copy.start()

    @pl.when(step + 1 < steps)
    def _():
        for copy in copies(step + 1, lax.rem(step + 1, 2)):
            copy.start()

    slot = lax.rem(step, 2)
    for copy in copies(step, slot):
        copy.wait()
    gate_tile = matmul(left[...], held[slot, 0])
    gate[...] = gate_tile
    up_tile = matmul(left[...], held[slot, 1])
    up[...] = up_tile
    value = (gate_tile * jax.nn.sigmoid(gate_tile) * up_tile).astype(hidden.dtype)
    hidden[...] = value
    turned[...] = value.T


def gate_up(left, gates, ups):
    count, (rows, columns) = len(gates), gates[0].shape
    tokens = left.shape[0]
    tile = next(size for size in (512, 256, 128) if columns % size == 0)
    across = pl.BlockSpec((tokens, tile), lambda step: (0, step))
    return pl.pallas_call(
        functools.partial(gate_kernel, count),
        out_shape=[
            jax.ShapeDtypeStruct((tokens, columns), jnp.float32),
            jax.ShapeDtypeStruct((tokens, columns), jnp.float32),
            jax.ShapeDtypeStruct((tokens, columns), left.dtype),
            jax.ShapeDtypeStruct((columns, tokens), left.dtype),
        ],
        grid=(columns // tile,),
        in_specs=[pl.BlockSpec(left.shape, lambda step: (0, 0))] + [ANYWHERE] * (2 * count),
        out_specs=[across, across, across, pl.BlockSpec((tile, tokens), lambda step: (step, 0))],
        scratch_shapes=[
            pltpu.VMEM((2, 2, count * rows, tile), left.dtype),
            pltpu.SemaphoreType.DMA((2, 2, count)),
        ],
        **kernel_params(
            4 * tokens * count * rows * columns, 4 * columns * (count * rows + 3 * tokens)
        ),
    )(left, *[held[place] for held in (gates, ups) for place in range(count)])


def turn_kernel(source, out):
    out[...] = source[...].T


def turned_over(source):
    rows, columns = source.shape
    return pl.pallas_call(
        turn_kernel,
        out_shape=jax.ShapeDtypeStruct((columns, rows), source.dtype),
        grid=(columns // 512,),
        in_specs=[pl.BlockSpec((rows, 512), lambda step: (0, step))],
        out_specs=pl.BlockSpec((512, rows), lambda step: (step, 0)),
        **kernel_params(0, 4 * rows * columns),
    )(source)


def down_kernel(count, together, sides, back, near, *refs):
    if back:
        gate, up, cot = refs[:3]
        refs = refs[3:]
    else:
        hidden, mid = refs[:2]
        refs = refs[2:]
    own, other = refs[:2]
    halves = len(sides) - 1
    pieces = refs[2 : 2 + halves * count]
    if back:
        grad_gate, grad_up, held, sems = refs[2 + halves * count :]
    else:
        output, held, total, sems = refs[2 + halves * count :]
    step, steps = pl.program_id(0), pl.num_programs(0)
    rows = own.shape[1]

    def copies(number, slot):
        for part in range(together):
            spot = lax.rem(owner(part), together)
            start = pl.multiple_of(spot * rows, rows)
            place = number * together + part
            sources = [(other if place & 1 else own).at[place >> 1]]
            sources += [pieces[half * count + place] for half in range(halves)]
            for which, (left, right) in enumerate(sides):
                yield pltpu.make_async_copy(
                    sources[which],
                    held.at[slot, pl.ds(start, rows), left:right],
                    sems.at[slot, part, which],
                )

    for number in range(count // together):

        @pl.when(step == max(number - 1, 0))
        def _(number=number):
            for copy in copies(number, number % 2):
                copy.start()

    slot = lax.rem(step, 2)
    for copy in copies(0, slot):
        copy.wait()
    weight = held[slot]
    if back:
        grad = across_rows(cot[...], weight)
        gate_rows, up_rows = gate[...], up[...]
        sigma = jax.nn.sigmoid(gate_rows)
        grad_up[...] = (grad * (gate_rows * sigma)).astype(grad_up.dtype)
        grad_gate[...] = (grad * up_rows * (sigma * (1.0 + gate_rows * (1.0 - sigma)))).astype(
            grad_gate.dtype
        )
        return
    added = matmul(hidden[...], weight)

    @pl.when(step == 0)
    def _():
        total[...] = mid[...] + added

    @pl.when(step > 0)
    def _():
        total[...] += added

    @pl.when(step == steps - 1)
    def _():
        output[...] = total[...].astype(output.dtype)


def with_down(operands, early, helds, back):
    count, (blocks, rows, first) = len(helds[0]), early[0].shape
    tokens, width = operands[-1].shape
    ends = [0, first]
    for held in helds:
        ends.append(ends[-1] + held[0].shape[1])
    sides = tuple(zip(ends, ends[1:]))
    together = next(size for size in (2, 4, 8, 16) if size * rows % 128 == 0)
    tile = together * rows
    dp = lax.axis_index("dp")
    near = lax.bitwise_xor(
        lax.div(dp, together), jnp.arange(count // together, dtype=jnp.int32)
    )
    across = pl.BlockSpec((tokens, tile), lambda step, near: (0, near[step]))
    fixed = pl.BlockSpec((tokens, width), lambda step, near: (0, 0))
    columns = count * rows
    wide = jax.ShapeDtypeStruct((tokens, columns), jnp.bfloat16)
    scratch = [pltpu.VMEM((2, tile, width), jnp.bfloat16)]
    if not back:
        scratch.append(pltpu.VMEM((tokens, width), jnp.float32))
    scratch.append(pltpu.SemaphoreType.DMA((2, together, len(sides))))
    return pl.pallas_call(
        functools.partial(down_kernel, count, together, sides, back),
        out_shape=[wide, wide] if back else jax.ShapeDtypeStruct((tokens, width), jnp.bfloat16),
        grid_spec=pltpu.PrefetchScalarGridSpec(
            num_scalar_prefetch=1,
            grid=(count // together,),
            in_specs=([across, across, fixed] if back else [across, fixed])
            + [ANYWHERE] * (2 + len(helds) * count),
            out_specs=[across, across] if back else fixed,
            scratch_shapes=scratch,
        ),
        **kernel_params(2 * tokens * width * columns, 2 * columns * (width + 5 * tokens)),
    )(near, *operands, *early, *[held[place] for held in helds for place in range(count)])


class Flow:
    def __init__(self):
        self.ended = []

    def round(self, moves):
        values = after([value for value, _ in moves], self.ended)
        self.fence = values
        got = [
            bit(value) if callable(bit) else partner(value, bit)
            for value, (_, bit) in zip(values, moves)
        ]
        self.ended = list(got)
        return got

    def holds(self, *results):
        self.ended.extend(results)


def exchange(flow, jobs, also=()):
    moves = [job.moves() for job in jobs]
    got = flow.round([move for found in moves for move in found] + list(also))
    for job, found in zip(jobs, moves):
        job.receive(got[: len(found)])
        got = got[len(found) :]
    return got


class Order:
    def __init__(self):
        self.last = []

    def __call__(self, work, *operands):
        got = work(*after(operands, self.last))
        self.last = [got]
        return got

    def first(self, job):
        job.right = after(job.right, self.last)
        self.last = [job.first()]

    def send(self, job):
        job.right = after(job.right, self.last)
        self.last = list(job.send())

    def line(self, job):
        job.right = after(job.right, self.last)
        self.last = [job.line()]
        return self.last[0]


class Shallow:
    def __init__(self, shard, order):
        self.order, self.pieces, self.level = order, {0: shard}, 0

    def moves(self):
        self.level += 1
        self.places = [
            place
            for place in range(2 << len(self.order))
            if not place & 1 and bin(place).count("1") == self.level
        ]
        found = []
        for place in self.places:
            bit = next(bit for bit in self.order if place >> bit & 1)
            found.append((self.pieces[place ^ (1 << bit)], bit))
        return found

    def put(self, got):
        for place, piece in zip(self.places, got):
            self.pieces[place] = piece

    def left(self):
        return self.level < len(self.order)


class Spreads:
    def __init__(self, order):
        self.order, self.helds = order, [{}, {}]

    def direct(self, flow, number, line, also=()):
        held = self.helds[number]
        held[0] = line
        moves = [(line, 0)] + [(line, bit) for bit in self.order] + list(also)
        got = flow.round(moves)
        held[1] = got[0]
        for bit, piece in zip(self.order, got[1:]):
            held[1 << bit] = piece
        return got[1 + len(self.order) :]

    def both(self, flow, lines):
        got = flow.round([(line, bit) for line in lines for bit in self.order])
        for number, line in enumerate(lines):
            held = self.helds[number]
            held[0] = line
            for place, bit in enumerate(self.order):
                held[1 << bit] = got[number * len(self.order) + place]

    def double(self):
        return [
            (number, place)
            for number, held in enumerate(self.helds)
            for place in sorted(held)
            if not place & 1 and place | 1 not in held
        ]

    def moves(self, names):
        return [(self.helds[number][place], 0) for number, place in names]

    def put(self, names, got):
        for (number, place), piece in zip(names, got):
            self.helds[number][place | 1] = piece

    def cross(self, flow, level, also, cores):
        names, targets, moves = self.double() if cores else [], [], []
        for number, turn in enumerate((self.order, self.order[::-1])):
            for place in range(2 << len(self.order)):
                bits = [bit for bit in turn if place >> bit & 1]
                if not place & 1 and len(bits) == level:
                    targets.append((number, place))
                    moves.append((self.helds[number][place ^ (1 << bits[-1])], bits[-1]))
        got = flow.round(moves + self.moves(names) + list(also))
        for (number, place), piece in zip(targets, got):
            self.helds[number][place] = piece
        end = len(targets) + len(names)
        self.put(names, got[len(targets) : end])
        return got[end:]

    def crosses(self, flow, also=(), cores=True):
        extra = []
        for level in range(2, len(self.order) + 1):
            extra += self.cross(flow, level, also if level == 2 else (), cores)
        return extra


def places_of(order):
    places = [0]
    for bit in reversed(order):
        places = places + [place | (1 << bit) for place in places]
    return places


def sum_kernel(shared, each, table, turned, right, *refs):
    outs = refs[shared + 2 * each :]
    total = matmul(turned[...], right[...])
    for part in refs[:shared]:
        total = total + part[...].astype(jnp.float32)
    sides = 2 if len(outs) == 2 or each else 1
    for side in range(sides):

        @pl.when(pl.program_id(0) == side)
        def _(side=side):
            mine = total
            for part in refs[shared + side * each : shared + (side + 1) * each]:
                mine = mine + part[...].astype(jnp.float32)
            out = outs[side % len(outs)]
            out[...] = mine.astype(out.dtype)


def summed_rows(turned, right, rows, shared=(), parts=((), ()), apart=False):
    sides, count = len(rows), len(rows[0])
    tokens, columns = right.shape[0], right.shape[1] // sides
    block = turned.shape[0] // lax.axis_size("dp")
    table = [[place for side in rows for place in side]]
    table += [[places.index(place) for side in rows for place in side] for _, places in shared]
    for side in range(sides):
        table += [[places.index(place) for place in rows[side]] * sides for _, places in parts[side]]
    spots = jnp.array(table, jnp.int32)
    spots = spots.at[0].set(lax.bitwise_xor(spots[0], lax.axis_index("dp")))
    each = len(parts[0])

    def shared_spec(line):
        return pl.BlockSpec(
            (block, columns),
            lambda now, step, spots: (spots[line, now * count + step], now),
        )

    def one_side(side, row):
        def index(now, step, spots):
            step = jnp.where(now == side, step, jnp.where(now < side, 0, count - 1))
            return (row(step, spots), 0)

        return pl.BlockSpec((block, columns), index)

    def part_spec(side, line):
        return one_side(side, lambda step, spots: spots[line, step])

    if apart:
        out_shape = [jax.ShapeDtypeStruct((count * block, columns), jnp.bfloat16)] * sides
        out_specs = [one_side(side, lambda step, spots: step) for side in range(sides)]
    else:
        out_shape = [jax.ShapeDtypeStruct((count * block, sides * columns), jnp.bfloat16)]
        out_specs = [pl.BlockSpec((block, columns), lambda now, step, spots: (step, now))]
    base = 1 + len(shared)
    return pl.pallas_call(
        functools.partial(sum_kernel, len(shared), each),
        out_shape=out_shape,
        grid_spec=pltpu.PrefetchScalarGridSpec(
            num_scalar_prefetch=1,
            grid=(sides, count),
            in_specs=[
                pl.BlockSpec(
                    (block, tokens),
                    lambda now, step, spots: (spots[0, now * count + step], 0),
                ),
                pl.BlockSpec((tokens, columns), lambda now, step, spots: (0, now)),
            ]
            + [shared_spec(1 + number) for number in range(len(shared))]
            + [
                part_spec(side, base + side * each + number)
                for side in range(sides)
                for number in range(each)
            ],
            out_specs=out_specs,
        ),
        **kernel_params(
            2 * tokens * sides * count * block * columns,
            2 * sides * count * block * columns * (1 + len(shared) + each),
        ),
    )(spots, turned, right, *[part for part, _ in shared], *[p for side in parts for p, _ in side])


class Pair:
    def __init__(self, turned, right, order):
        self.turned, self.right = turned, right
        self.orders = (order, order[::-1])
        self.kept = [places_of(turn) for turn in self.orders]
        self.whole = places_of(order)
        self.shared, self.parts, self.step = [], ([], []), 0

    def first(self):
        places = [place | 1 for place in self.whole]
        self.sent = summed_rows(self.turned, self.right, [places])
        return self.sent[0]

    def first_move(self):
        return (self.sent[0], 0)

    def first_receive(self, got):
        self.shared = [(got, self.whole)]

    def send(self):
        half = len(self.kept[0]) // 2
        self.sent = summed_rows(
            self.turned,
            self.right,
            [kept[half:] for kept in self.kept],
            self.shared,
            self.parts,
            apart=True,
        )
        self.kept = [kept[:half] for kept in self.kept]
        return self.sent

    def moves(self):
        return [(sent, turn[self.step]) for sent, turn in zip(self.sent, self.orders)]

    def receive(self, got):
        for piece, parts, kept in zip(got, self.parts, self.kept):
            parts.append((piece, kept))
        self.step += 1

    def left(self):
        return len(self.orders[0]) - self.step

    def line(self):
        self.sent = summed_rows(self.turned, self.right, self.kept, self.shared, self.parts)
        return self.sent[0]


def finish(line):
    return lax.psum_scatter(line, "seq", scatter_dimension=0, tiled=True).astype(jnp.float32)


class Halved:
    def __init__(self, blocks, order):
        self.order, self.step = order, 0
        self.kept = [block.astype(jnp.float32) for block in blocks]

    def left(self):
        return len(self.order) - self.step

    def moves(self):
        half = len(self.kept) // 2
        sent = jnp.concatenate(self.kept[half:], axis=0).astype(jnp.bfloat16)
        self.kept = self.kept[:half]
        return [(sent, self.order[self.step])]

    def receive(self, got):
        (got,) = got
        rows = got.shape[0] // len(self.kept)
        self.kept = [
            kept + got[number * rows : (number + 1) * rows].astype(jnp.float32)
            for number, kept in enumerate(self.kept)
        ]
        self.step += 1


def on_device(
    tokens,
    lengths,
    gain_one,
    w_query,
    w_key,
    w_value,
    w_out,
    gain_two,
    w_gate,
    w_up,
    w_down,
    cotangent,
):
    half_type = jnp.bfloat16
    batch, group, width = tokens.shape
    count = batch * group
    upper = tuple(range(1, dp_bits()))
    inner = w_query.shape[1]
    middle = w_down.shape[1] // 2

    def along(shard):
        return lax.all_gather(shard, "seq", axis=0, tiled=True)

    gains = jnp.stack([gain_one, gain_two], axis=1)
    first = jnp.concatenate(
        [w_query, w_key, w_value, jnp.pad(gains, ((0, 0), (0, HEAD - 2)))], axis=1
    ).astype(half_type)
    columns_first = inner + 2 * HEAD
    flow = Flow()
    line_first = along(first)
    line_out = along(after(w_out.astype(half_type), line_first))
    one_spread, two_spread, three_spread = Spreads(upper), Spreads(upper), Spreads(upper)
    one_spread.direct(flow, 0, line_first)
    line_gate = along(after(w_gate.astype(half_type), line_out, flow.ended))
    line_up = along(after(w_up.astype(half_type), line_gate))
    down_half = w_down.astype(half_type)
    quarter = middle + middle // 2
    line_right = along(after(down_half[:, middle:], line_up))
    early_spread = Shallow(down_half[:, :middle], upper)
    flow.holds(line_out)
    early_spread.put(one_spread.direct(flow, 1, line_out, early_spread.moves()))
    one_spread.crosses(flow)
    flow.holds(line_gate)
    left_over = one_spread.double()
    one_spread.put(
        left_over, two_spread.direct(flow, 0, line_gate, one_spread.moves(left_over))
    )
    full_one = one_spread.helds

    reach = (WINDOW - 2) // group + 1
    offset = lax.axis_index("seq") * group
    query_at = offset + jnp.arange(group, dtype=jnp.int32)
    key_at = offset - reach * group + jnp.arange((reach + 1) * group, dtype=jnp.int32)
    query_seg, query_pos = documents(lengths, query_at)
    key_seg = documents(lengths, key_at)[0]
    allowed = (
        (key_at[None, :] >= 0)
        & (query_at[:, None] >= key_at[None, :])
        & (query_at[:, None] - key_at[None, :] < WINDOW)
    )
    allowed = allowed & (query_seg[0][:, None] == key_seg[0][None, :])
    bias = jnp.where(allowed.T, 0.0, -1e30)
    cosine, sine = rope_tables(query_pos)
    rows = tokens.astype(jnp.float32).reshape(count, width)
    scale_one = lax.rsqrt(jnp.mean(rows * rows, axis=-1, keepdims=True) + EPS)
    mapped, normed, gain_rows = by_rows(rows * scale_one, full_one[0], columns_first)
    gain_a, gain_b = gain_rows[0], gain_rows[1]
    query = mapped[:, :inner].reshape(batch, group, HEADS, HEAD)
    key = mapped[:, inner : inner + HEAD].reshape(batch, group, HEAD)
    value = mapped[:, inner + HEAD :].astype(half_type).reshape(batch, group, HEAD)
    query_turned = rotate(query, cosine[:, :, None, :], sine[:, :, None, :]).astype(half_type)
    key_turned = rotate(key, cosine, sine).astype(half_type)
    paired = jnp.concatenate([key_turned, value], axis=-1)
    pieces = []
    for step in range(reach, 0, -1):
        pieces.append(shifted(paired, "seq", step))
    pieces.append(paired)
    seen = jnp.concatenate(pieces, axis=1)
    keys_seen = seen[..., :HEAD]
    values_seen = seen[..., HEAD:]

    query_turned = query_turned.reshape(count, HEADS * HEAD)
    keys_seen, values_seen = keys_seen[0], values_seen[0]
    flow.holds(line_up, query_turned)
    early_spread.put(two_spread.direct(flow, 1, line_up, early_spread.moves()))
    while early_spread.left():
        early_spread.put(flow.round(early_spread.moves()))
    places = sorted(early_spread.pieces)
    early = jnp.stack([early_spread.pieces[place] for place in places])
    early = lax.all_gather(after(early, line_right), "seq", axis=1, tiled=True)
    mixed, log_total = attend(bias, query_turned, keys_seen, values_seen.T)
    mid = rows + by_rows(mixed, full_one[1], width)[0]
    scale_two = lax.rsqrt(jnp.mean(mid * mid, axis=-1, keepdims=True) + EPS)
    normed_two = (mid * scale_two * gain_b).astype(half_type)

    turned_one, turned_mixed, turned_two = map(turned_over, (normed, mixed, normed_two))
    flow.holds(normed_two, line_right, turned_one, turned_mixed, turned_two)
    two_spread.crosses(flow)
    left_over = two_spread.double()
    lines_three = [line_right[:, : quarter - middle], line_right[:, quarter - middle :]]
    got = flow.round(two_spread.moves(left_over) + [(line, 0) for line in lines_three])
    two_spread.put(left_over, got)
    for held, piece in zip(three_spread.helds, got[len(left_over) :]):
        held[1] = piece
    full_two = two_spread.helds
    three_spread.both(flow, lines_three)
    order = Order()
    gate, up_val, hidden, hidden_turned = order(
        lambda left: gate_up(left, *full_two), normed_two
    )

    grad_out = cotangent.reshape(count, width)
    flow.holds(order.last)
    early = [early] + three_spread.crosses(flow, [(early, 0)], False)
    job_down = Pair(hidden_turned, grad_out, upper)
    order.first(job_down)
    flow.holds(order.last)
    left_over = three_spread.double()
    three_spread.put(left_over, flow.round(three_spread.moves(left_over)))
    job_down.first_receive(partner(after(job_down.sent[0], flow.ended), 0))
    full_three = three_spread.helds
    grad_gate, grad_up = order(
        lambda *operands: with_down(operands, early, full_three, True), gate, up_val, grad_out
    )
    job_gate = Pair(turned_two, grad_gate, upper)
    job_up = Pair(turned_two, grad_up, upper)

    def rest(job):
        while job.left() > 1:
            order.send(job)
            exchange(flow, [job])

    order.first(job_gate)
    job_gate.first_receive(partner(*job_gate.first_move()))
    order.first(job_up)
    job_down.right = after(job_down.right, order.last)
    order.last = summed_rows(job_down.turned, job_down.right, [job_down.whole], job_down.shared)
    down_parts = lax.psum_scatter(
        order.last[0].reshape(len(places), -1, width), "seq", scatter_dimension=1, tiled=True
    )
    sums = []
    for turn, part in (
        (upper, down_parts[:, :, :middle]),
        (upper[::-1], down_parts[:, :, middle:]),
    ):
        sums.append(Halved([part[job_down.whole.index(place)] for place in places_of(turn)], turn))
    order.send(job_gate)
    flow.holds(order.last)
    job_up.first_receive(exchange(flow, [job_gate], [job_up.first_move()])[0])

    grad_normed_two = order(
        lambda *lefts: back_by_rows(lefts, full_two, jnp.float32), grad_gate, grad_up
    )
    back_mid, gain_two_term = norm_back(grad_normed_two, mid, scale_two, gain_b)
    grad_mid = grad_out.astype(jnp.float32) + back_mid
    grad_branch = grad_mid.astype(half_type)
    job_out = Pair(turned_mixed, grad_branch, upper)
    order.last = [grad_branch]
    order.first(job_out)
    order.send(job_up)
    flow.holds(order.last)
    job_out.first_receive(exchange(flow, [job_up], [job_out.first_move()])[0])

    rest(job_gate)
    order.send(job_gate)
    grad_mixed = order(lambda left: back_by_rows([left], full_one[1:], half_type), grad_branch)
    grad_q, grad_keys, grad_values = order(
        lambda left: attend_back(
            bias, cosine[0].T, sine[0].T, query_turned, left, log_total, keys_seen, values_seen
        ),
        grad_mixed,
    )
    flow.holds(order.last)
    exchange(flow, [job_gate])

    grad_seen = jnp.concatenate([grad_keys, grad_values], axis=-1)[None]
    own, arrived = grad_seen[:, reach * group :], []
    for step in range(1, reach + 1):
        part = grad_seen[:, (reach - step) * group : (reach - step + 1) * group]
        part = shifted(part.astype(jnp.bfloat16), "seq", -step)
        arrived.append(part)
        own = own + part.astype(own.dtype)
    grad_key = rotate(own[..., :HEAD], cosine, -sine).astype(half_type).reshape(count, HEAD)
    grad_value = own[..., HEAD:].astype(half_type).reshape(count, HEAD)
    rest(job_up)
    order.send(job_up)
    output = order(
        lambda *operands: with_down(operands, early, full_three, False), hidden, mid
    ).reshape(batch, group, width)
    flow.holds(order.last)
    exchange(flow, [job_up])

    gate_done = finish(order.line(job_gate))
    grad_first = jnp.concatenate([grad_q, grad_key, grad_value], axis=1)
    job_first = Pair(turned_one, grad_first, upper)
    order.first(job_first)
    job_first.first_receive(partner(*job_first.first_move()))
    order.send(job_out)
    flow.holds(order.last)
    exchange(flow, [job_out])

    up_done = finish(order.line(job_up))
    order.send(job_first)
    flow.holds(order.last, down_parts)
    exchange(flow, [job_first])

    rest(job_out)
    order.send(job_out)
    grad_normed = order(
        lambda left: back_by_rows([left], full_one[:1], jnp.float32), grad_first
    )
    flow.holds(order.last)
    exchange(flow, [job_out])

    rest(job_first)
    order.send(job_first)
    flow.holds(order.last)
    exchange(flow, [job_first])
    grad_normed = after(grad_normed, flow.fence)
    back_rows, gain_one_term = norm_back(grad_normed, rows, scale_one, gain_a)
    grad_rows = (grad_mid + back_rows).astype(half_type).reshape(batch, group, width)
    gain_terms = jnp.stack([gain_one_term, gain_two_term])

    out_done = finish(order.line(job_out))
    first_done = finish(order.line(job_first))
    flow.holds(order.last)
    while sums[0].left():
        exchange(flow, sums)
    down_done = jnp.concatenate([part.kept[0] for part in sums], axis=1)
    bits = range(dp_bits())
    for bit in bits:
        gain_terms = gain_terms + partner(gain_terms, bit)
    gain_terms = sum(
        [around(gain_terms, steps) for steps in range(1, lax.axis_size("seq"))], gain_terms
    )
    owned = gain_one.shape[0]
    mine = (lax.axis_index("dp") * lax.axis_size("seq") + lax.axis_index("seq")) * owned
    gain_done = lax.dynamic_slice_in_dim(gain_terms, mine, owned, 1)
    return (
        output,
        grad_rows,
        gain_done[0],
        first_done[:, :inner],
        first_done[:, inner : inner + HEAD],
        first_done[:, inner + HEAD :],
        out_done,
        gain_done[1],
        gate_done,
        up_done,
        down_done,
    )


def solution(mesh):
    in_specs = (
        P("dp", "seq", None),
        P("dp", None),
        P(("dp", "seq")),
        P(("dp", "seq"), None),
        P(("dp", "seq"), None),
        P(("dp", "seq"), None),
        P(("dp", "seq"), None),
        P(("dp", "seq")),
        P(("dp", "seq"), None),
        P(("dp", "seq"), None),
        P(("dp", "seq"), None),
        P("dp", "seq", None),
    )
    out_specs = (
        P("dp", "seq", None),
        P("dp", "seq", None),
        P(("dp", "seq")),
        P(("dp", "seq"), None),
        P(("dp", "seq"), None),
        P(("dp", "seq"), None),
        P(("dp", "seq"), None),
        P(("dp", "seq")),
        P(("dp", "seq"), None),
        P(("dp", "seq"), None),
        P(("dp", "seq"), None),
    )
    return jax.shard_map(
        on_device, mesh=mesh, in_specs=in_specs, out_specs=out_specs, check_vma=False
    )
```

```python
import functools
import math

import jax
import jax.numpy as jnp
from jax import lax
from jax.experimental import pallas as pl
from jax.experimental.pallas import tpu as pltpu
from jax.sharding import PartitionSpec as P

HEADS = 16
HEAD = 128
WINDOW = 512


EPS = 1e-05


def shifted(value, axis, steps):
    count = lax.axis_size(axis)
    initial, last = (max(0, -steps), min(count, count - steps))
    return lax.ppermute(value, axis, [(source, source + steps) for source in range(initial, last)])


def documents(doc_lengths, index):
    ends = jnp.cumsum(doc_lengths, axis=-1)
    passed = (index[None, :, None] >= ends[:, None, :]).astype(jnp.int32)
    segment = jnp.sum(passed, axis=-1)
    before = jnp.sum(passed * doc_lengths[:, None, :], axis=-1)
    return (segment, index[None, :] - before)


def rope_tables(position):
    half = HEAD // 2
    freq = jnp.exp(jnp.arange(half, dtype=jnp.float32) * (-2.0 * math.log(10000.0) / HEAD))
    angles = position.astype(jnp.float32)[..., None] * freq
    return (jnp.cos(angles), jnp.sin(angles))


def rotate(vec, cosine, sine):
    half = vec.shape[-1] // 2
    first = vec[..., :half]
    second = vec[..., half:]
    return jnp.concatenate(
        [first * cosine - second * sine, second * cosine + first * sine], axis=-1
    )


def norm_back(grad_normed, rows, scale, gain):
    inner = grad_normed * gain
    grad_gain = jnp.sum(grad_normed * rows * scale, axis=0)
    grad_rows = scale * inner - rows * (scale * scale * scale) * jnp.mean(
        inner * rows, axis=-1, keepdims=True
    )
    return (grad_rows, grad_gain)


def matmul(left, right):
    return jnp.dot(left, right, preferred_element_type=jnp.float32)


def after(values, *others):
    return lax.optimization_barrier((values, others))[0]


def partner(value, bit):
    count = lax.axis_size("dp")
    return lax.ppermute(value, "dp", [(source, source ^ (1 << bit)) for source in range(count)])


def around(value, steps):
    count = lax.axis_size("seq")
    return lax.ppermute(
        value, "seq", [(source, (source + steps) % count) for source in range(count)]
    )


def dp_bits():
    return lax.axis_size("dp").bit_length() - 1


MIB = 1 << 20
STREAMS = 4
ANYWHERE = pl.BlockSpec(memory_space=pl.ANY)


def kernel_params(flops, traffic):
    return {
        "compiler_params": pltpu.CompilerParams(vmem_limit_bytes=58 * MIB),
        "cost_estimate": pl.CostEstimate(
            flops=flops, bytes_accessed=traffic, transcendentals=0
        ),
    }


def owner(number):
    return lax.bitwise_xor(lax.axis_index("dp"), number)


def rows_kernel(count, gained, near, left, *refs):
    pieces, rest = refs[:count], refs[count:]
    if gained:
        out, normed, gains, held, sems = rest
    else:
        out, held, sems = rest
    step = pl.program_id(0)
    rows, columns = held.shape[1], out.shape[1]
    copies = [
        pltpu.make_async_copy(piece, held.at[number], sems.at[number])
        for number, piece in enumerate(pieces)
    ]

    @pl.when(step == 0)
    def _():
        for copy in copies:
            copy.start()

    for number, copy in enumerate(copies):

        @pl.when(step == number)
        def _(copy=copy):
            copy.wait()

    start = pl.multiple_of(owner(step) * rows, rows)
    block = left[:, pl.ds(start, rows)]
    if gained:
        turned = held[step, :, columns:].astype(jnp.float32).T
        gains[...] = turned[:8]
        block = (block * turned[:1]).astype(normed.dtype)
        normed[...] = block
    part = matmul(block, held[step, :, :columns])

    @pl.when(step == 0)
    def _():
        out[...] = part

    @pl.when(step > 0)
    def _():
        out[...] += part


def near_places(count):
    return lax.bitwise_xor(lax.axis_index("dp"), jnp.arange(count, dtype=jnp.int32))


def by_rows(left, held, columns):
    count, (rows, wide) = len(held), held[0].shape
    tokens = left.shape[0]
    gained = wide > columns
    out_shape = [jax.ShapeDtypeStruct((tokens, columns), jnp.float32)]
    out_specs = [pl.BlockSpec((tokens, columns), lambda step, near: (0, 0))]
    if gained:
        out_shape += [
            jax.ShapeDtypeStruct(left.shape, held[0].dtype),
            jax.ShapeDtypeStruct((8, left.shape[1]), jnp.float32),
        ]
        out_specs += [
            pl.BlockSpec((tokens, rows), lambda step, near: (0, near[step])),
            pl.BlockSpec((8, rows), lambda step, near: (0, near[step])),
        ]
    return pl.pallas_call(
        functools.partial(rows_kernel, count, gained),
        out_shape=out_shape,
        grid_spec=pltpu.PrefetchScalarGridSpec(
            num_scalar_prefetch=1,
            grid=(count,),
            in_specs=[pl.BlockSpec(left.shape, lambda step, near: (0, 0))] + [ANYWHERE] * count,
            out_specs=out_specs,
            scratch_shapes=[
                pltpu.VMEM((count, rows, wide), held[0].dtype),
                pltpu.SemaphoreType.DMA((count,)),
            ],
        ),
        **kernel_params(2 * tokens * count * rows * columns, 2 * count * rows * columns),
    )(near_places(count), left, *[held[place] for place in range(count)])


def back_kernel(count, many, near, *refs):
    lefts = refs[:many]
    pieces = refs[many : many + many * count]
    out, held, sems = refs[many + many * count :]
    step = pl.program_id(0)

    rows = held.shape[2]
    share = rows // STREAMS

    def copies(number, slot):
        for which in range(many):
            for stream in range(STREAMS):
                part = pl.ds(stream * share, share)
                yield pltpu.make_async_copy(
                    pieces[which * count + number].at[part, :],
                    held.at[slot, which, part, :],
                    sems.at[slot, which, stream],
                )

    for number in range(count):

        @pl.when(step == max(number - 1, 0))
        def _(number=number):
            for copy in copies(number, number % 2):
                copy.start()

    slot = lax.rem(step, 2)
    for copy in copies(0, slot):
        copy.wait()
    total = None
    for which in range(many):
        part = lax.dot_general(
            lefts[which][...],
            held[slot, which, :, : lefts[which].shape[1]],
            (((1,), (1,)), ((), ())),
            preferred_element_type=jnp.float32,
        )
        total = part if total is None else total + part
    out[...] = total.astype(out.dtype)


def back_by_rows(lefts, helds, dtype):
    count, many = len(helds[0]), len(lefts)
    rows, wide = helds[0][0].shape
    tokens, columns = lefts[0].shape
    near = near_places(count)
    return pl.pallas_call(
        functools.partial(back_kernel, count, many),
        out_shape=jax.ShapeDtypeStruct((tokens, count * rows), dtype),
        grid_spec=pltpu.PrefetchScalarGridSpec(
            num_scalar_prefetch=1,
            grid=(count,),
            in_specs=[pl.BlockSpec((tokens, columns), lambda step, near: (0, 0))] * many
            + [ANYWHERE] * (many * count),
            out_specs=pl.BlockSpec((tokens, rows), lambda step, near: (0, near[step])),
            scratch_shapes=[
                pltpu.VMEM((2, many, rows, wide), helds[0][0].dtype),
                pltpu.SemaphoreType.DMA((2, many, STREAMS)),
            ],
        ),
        **kernel_params(
            2 * tokens * many * count * rows * columns, 2 * many * count * rows * columns
        ),
    )(near, *lefts, *[held[place] for held in helds for place in range(count)])


def across_rows(left, right):
    return lax.dot_general(
        left, right, (((1,), (1,)), ((), ())), preferred_element_type=jnp.float32
    )


def attend_kernel(bias, query, keys, values_turned, mixed, log_total):
    block = min(256, query.shape[0])
    for number in range(query.shape[0] // block):
        mine = slice(number * block, (number + 1) * block)
        seen = slice(number * block, (number + 1) * block + WINDOW)
        scores = across_rows(keys[seen, :], query[mine, :]) * (1.0 / math.sqrt(HEAD))
        scores = scores + bias[seen, mine]
        top = jnp.max(scores, axis=0, keepdims=True)
        weight = jnp.exp(scores - top)
        total = jnp.sum(weight, axis=0, keepdims=True)
        probs = (weight * (1.0 / total)).astype(jnp.bfloat16)
        mixed[mine, :] = matmul(values_turned[:, seen], probs).T.astype(mixed.dtype)
        log_total[0, :, mine] = top + jnp.log(total)


def head_specs(group, length):
    def whole(*shape):
        return pl.BlockSpec(shape, lambda head: (0, 0))

    column = pl.BlockSpec((group, HEAD), lambda head: (0, head))
    row = pl.BlockSpec((1, 1, group), lambda head: (head, 0, 0))
    return whole, column, row


def attend(bias, query, keys, values_turned):
    length, group = bias.shape
    whole, column, row = head_specs(group, length)
    heads = query.shape[1] // HEAD
    return pl.pallas_call(
        attend_kernel,
        out_shape=[
            jax.ShapeDtypeStruct(query.shape, query.dtype),
            jax.ShapeDtypeStruct((heads, 1, group), jnp.float32),
        ],
        grid=(heads,),
        in_specs=[whole(length, group), column, whole(length, HEAD), whole(HEAD, length)],
        out_specs=[column, row],
        **kernel_params(4 * length * query.shape[0] * query.shape[1], 8 * query.size),
    )(bias, query, keys, values_turned)


def attend_back_kernel(
    bias, cosine, sine, query, grad_mixed, log_total, keys, keys_turned, values, grad_query,
    grad_keys, grad_values,
):
    block = min(256, query.shape[0])
    factor = 1.0 / math.sqrt(HEAD)

    @pl.when(pl.program_id(0) == 0)
    def _():
        grad_keys[...] = jnp.zeros_like(grad_keys)
        grad_values[...] = jnp.zeros_like(grad_values)

    for number in range(query.shape[0] // block):
        mine = slice(number * block, (number + 1) * block)
        seen = slice(number * block, (number + 1) * block + WINDOW)
        query_rows, grad_rows = query[mine, :], grad_mixed[mine, :]
        scores = across_rows(keys[seen, :], query_rows) * factor + bias[seen, mine]
        probs = jnp.exp(scores - log_total[0, :, mine])
        grad_probs = across_rows(values[seen, :], grad_rows)
        centre = jnp.sum(probs * grad_probs, axis=0, keepdims=True)
        grad_scores = (probs * (grad_probs - centre)).astype(jnp.bfloat16)
        grad_keys[seen, :] += matmul(grad_scores, query_rows) * factor
        grad_values[seen, :] += matmul(probs.astype(jnp.bfloat16), grad_rows)
        turned = matmul(keys_turned[:, seen], grad_scores) * factor
        first, second = turned[: HEAD // 2], turned[HEAD // 2 :]
        cos, sin = cosine[:, mine], sine[:, mine]
        grad_query[mine, :HEAD // 2] = (first * cos + second * sin).T.astype(grad_query.dtype)
        grad_query[mine, HEAD // 2 :] = (second * cos - first * sin).T.astype(grad_query.dtype)


def attend_back(bias, cosine, sine, query, grad_mixed, log_total, keys, values):
    length, group = bias.shape
    whole, column, row = head_specs(group, length)
    heads = query.shape[1] // HEAD
    half = whole(HEAD // 2, group)
    return pl.pallas_call(
        attend_back_kernel,
        out_shape=[
            jax.ShapeDtypeStruct(query.shape, query.dtype),
            jax.ShapeDtypeStruct((length, HEAD), jnp.float32),
            jax.ShapeDtypeStruct((length, HEAD), jnp.float32),
        ],
        grid=(heads,),
        in_specs=[whole(length, group), half, half, column, column, row]
        + [whole(length, HEAD), whole(HEAD, length), whole(length, HEAD)],
        out_specs=[column, whole(length, HEAD), whole(length, HEAD)],
        **kernel_params(10 * length * query.shape[0] * query.shape[1], 12 * query.size),
    )(bias, cosine, sine, query, grad_mixed, log_total, keys, keys.T, values)


def gate_kernel(count, left, *refs):
    pieces = refs[: 2 * count]
    gate, up, hidden, turned, held, sems = refs[2 * count :]
    step, steps = pl.program_id(0), pl.num_programs(0)
    rows, tile = pieces[0].shape[0], gate.shape[1]

    def copies(number, slot):
        column = pl.multiple_of(number * tile, tile)
        for which in range(2):
            for place in range(count):
                start = pl.multiple_of(owner(place) * rows, rows)
                yield pltpu.make_async_copy(
                    pieces[which * count + place].at[:, pl.ds(column, tile)],
                    held.at[slot, which, pl.ds(start, rows), :],
                    sems.at[slot, which, place],
                )

    @pl.when(step == 0)
    def _():
        for copy in copies(0, 0):
            copy.start()

    @pl.when(step + 1 < steps)
    def _():
        for copy in copies(step + 1, lax.rem(step + 1, 2)):
            copy.start()

    slot = lax.rem(step, 2)
    for copy in copies(step, slot):
        copy.wait()
    gate_tile = matmul(left[...], held[slot, 0])
    gate[...] = gate_tile
    up_tile = matmul(left[...], held[slot, 1])
    up[...] = up_tile
    value = (gate_tile * jax.nn.sigmoid(gate_tile) * up_tile).astype(hidden.dtype)
    hidden[...] = value
    turned[...] = value.T


def gate_up(left, gates, ups):
    count, (rows, columns) = len(gates), gates[0].shape
    tokens = left.shape[0]
    tile = next(size for size in (512, 256, 128) if columns % size == 0)
    across = pl.BlockSpec((tokens, tile), lambda step: (0, step))
    return pl.pallas_call(
        functools.partial(gate_kernel, count),
        out_shape=[
            jax.ShapeDtypeStruct((tokens, columns), jnp.float32),
            jax.ShapeDtypeStruct((tokens, columns), jnp.float32),
            jax.ShapeDtypeStruct((tokens, columns), left.dtype),
            jax.ShapeDtypeStruct((columns, tokens), left.dtype),
        ],
        grid=(columns // tile,),
        in_specs=[pl.BlockSpec(left.shape, lambda step: (0, 0))] + [ANYWHERE] * (2 * count),
        out_specs=[across, across, across, pl.BlockSpec((tile, tokens), lambda step: (step, 0))],
        scratch_shapes=[
            pltpu.VMEM((2, 2, count * rows, tile), left.dtype),
            pltpu.SemaphoreType.DMA((2, 2, count)),
        ],
        **kernel_params(
            4 * tokens * count * rows * columns, 4 * columns * (count * rows + 3 * tokens)
        ),
    )(left, *[held[place] for held in (gates, ups) for place in range(count)])


def turn_kernel(source, out):
    out[...] = source[...].T


def turned_over(source):
    rows, columns = source.shape
    return pl.pallas_call(
        turn_kernel,
        out_shape=jax.ShapeDtypeStruct((columns, rows), source.dtype),
        grid=(columns // 512,),
        in_specs=[pl.BlockSpec((rows, 512), lambda step: (0, step))],
        out_specs=pl.BlockSpec((512, rows), lambda step: (step, 0)),
        **kernel_params(0, 4 * rows * columns),
    )(source)


def down_kernel(count, together, sides, back, near, *refs):
    if back:
        gate, up, cot = refs[:3]
        refs = refs[3:]
    else:
        hidden, mid = refs[:2]
        refs = refs[2:]
    own, other = refs[:2]
    halves = len(sides) - 1
    pieces = refs[2 : 2 + halves * count]
    if back:
        grad_gate, grad_up, held, sems = refs[2 + halves * count :]
    else:
        output, held, total, sems = refs[2 + halves * count :]
    step, steps = pl.program_id(0), pl.num_programs(0)
    rows = own.shape[1]

    def copies(number, slot):
        for part in range(together):
            spot = lax.rem(owner(part), together)
            start = pl.multiple_of(spot * rows, rows)
            place = number * together + part
            sources = [(other if place & 1 else own).at[place >> 1]]
            sources += [pieces[half * count + place] for half in range(halves)]
            for which, (left, right) in enumerate(sides):
                yield pltpu.make_async_copy(
                    sources[which],
                    held.at[slot, pl.ds(start, rows), left:right],
                    sems.at[slot, part, which],
                )

    for number in range(count // together):

        @pl.when(step == max(number - 1, 0))
        def _(number=number):
            for copy in copies(number, number % 2):
                copy.start()

    slot = lax.rem(step, 2)
    for copy in copies(0, slot):
        copy.wait()
    weight = held[slot]
    if back:
        grad = across_rows(cot[...], weight)
        gate_rows, up_rows = gate[...], up[...]
        sigma = jax.nn.sigmoid(gate_rows)
        grad_up[...] = (grad * (gate_rows * sigma)).astype(grad_up.dtype)
        grad_gate[...] = (grad * up_rows * (sigma * (1.0 + gate_rows * (1.0 - sigma)))).astype(
            grad_gate.dtype
        )
        return
    added = matmul(hidden[...], weight)

    @pl.when(step == 0)
    def _():
        total[...] = mid[...] + added

    @pl.when(step > 0)
    def _():
        total[...] += added

    @pl.when(step == steps - 1)
    def _():
        output[...] = total[...].astype(output.dtype)


def with_down(operands, early, helds, back):
    count, (blocks, rows, first) = len(helds[0]), early[0].shape
    tokens, width = operands[-1].shape
    ends = [0, first]
    for held in helds:
        ends.append(ends[-1] + held[0].shape[1])
    sides = tuple(zip(ends, ends[1:]))
    together = next(size for size in (2, 4, 8, 16) if size * rows % 128 == 0)
    tile = together * rows
    dp = lax.axis_index("dp")
    near = lax.bitwise_xor(
        lax.div(dp, together), jnp.arange(count // together, dtype=jnp.int32)
    )
    across = pl.BlockSpec((tokens, tile), lambda step, near: (0, near[step]))
    fixed = pl.BlockSpec((tokens, width), lambda step, near: (0, 0))
    columns = count * rows
    wide = jax.ShapeDtypeStruct((tokens, columns), jnp.bfloat16)
    scratch = [pltpu.VMEM((2, tile, width), jnp.bfloat16)]
    if not back:
        scratch.append(pltpu.VMEM((tokens, width), jnp.float32))
    scratch.append(pltpu.SemaphoreType.DMA((2, together, len(sides))))
    return pl.pallas_call(
        functools.partial(down_kernel, count, together, sides, back),
        out_shape=[wide, wide] if back else jax.ShapeDtypeStruct((tokens, width), jnp.bfloat16),
        grid_spec=pltpu.PrefetchScalarGridSpec(
            num_scalar_prefetch=1,
            grid=(count // together,),
            in_specs=([across, across, fixed] if back else [across, fixed])
            + [ANYWHERE] * (2 + len(helds) * count),
            out_specs=[across, across] if back else fixed,
            scratch_shapes=scratch,
        ),
        **kernel_params(2 * tokens * width * columns, 2 * columns * (width + 5 * tokens)),
    )(near, *operands, *early, *[held[place] for held in helds for place in range(count)])


class Flow:
    def __init__(self):
        self.ended = []

    def round(self, moves):
        values = after([value for value, _ in moves], self.ended)
        self.fence = values
        got = [
            bit(value) if callable(bit) else partner(value, bit)
            for value, (_, bit) in zip(values, moves)
        ]
        self.ended = list(got)
        return got

    def holds(self, *results):
        self.ended.extend(results)


def exchange(flow, jobs, also=()):
    moves = [job.moves() for job in jobs]
    got = flow.round([move for found in moves for move in found] + list(also))
    for job, found in zip(jobs, moves):
        job.receive(got[: len(found)])
        got = got[len(found) :]
    return got


class Order:
    def __init__(self):
        self.last = []

    def __call__(self, work, *operands):
        got = work(*after(operands, self.last))
        self.last = [got]
        return got

    def first(self, job):
        job.right = after(job.right, self.last)
        self.last = [job.first()]

    def send(self, job):
        job.right = after(job.right, self.last)
        self.last = list(job.send())

    def line(self, job):
        job.right = after(job.right, self.last)
        self.last = [job.line()]
        return self.last[0]


class Shallow:
    def __init__(self, shard, order):
        self.order, self.pieces, self.level = order, {0: shard}, 0

    def moves(self):
        self.level += 1
        self.places = [
            place
            for place in range(2 << len(self.order))
            if not place & 1 and bin(place).count("1") == self.level
        ]
        found = []
        for place in self.places:
            bit = next(bit for bit in self.order if place >> bit & 1)
            found.append((self.pieces[place ^ (1 << bit)], bit))
        return found

    def put(self, got):
        for place, piece in zip(self.places, got):
            self.pieces[place] = piece

    def left(self):
        return self.level < len(self.order)


class Spreads:
    def __init__(self, order):
        self.order, self.helds = order, [{}, {}]

    def direct(self, flow, number, line, also=()):
        held = self.helds[number]
        held[0] = line
        moves = [(line, 0)] + [(line, bit) for bit in self.order] + list(also)
        got = flow.round(moves)
        held[1] = got[0]
        for bit, piece in zip(self.order, got[1:]):
            held[1 << bit] = piece
        return got[1 + len(self.order) :]

    def both(self, flow, lines):
        got = flow.round([(line, bit) for line in lines for bit in self.order])
        for number, line in enumerate(lines):
            held = self.helds[number]
            held[0] = line
            for place, bit in enumerate(self.order):
                held[1 << bit] = got[number * len(self.order) + place]

    def double(self):
        return [
            (number, place)
            for number, held in enumerate(self.helds)
            for place in sorted(held)
            if not place & 1 and place | 1 not in held
        ]

    def moves(self, names):
        return [(self.helds[number][place], 0) for number, place in names]

    def put(self, names, got):
        for (number, place), piece in zip(names, got):
            self.helds[number][place | 1] = piece

    def cross(self, flow, level, also, cores):
        names, targets, moves = self.double() if cores else [], [], []
        for number, turn in enumerate((self.order, self.order[::-1])):
            for place in range(2 << len(self.order)):
                bits = [bit for bit in turn if place >> bit & 1]
                if not place & 1 and len(bits) == level:
                    targets.append((number, place))
                    moves.append((self.helds[number][place ^ (1 << bits[-1])], bits[-1]))
        got = flow.round(moves + self.moves(names) + list(also))
        for (number, place), piece in zip(targets, got):
            self.helds[number][place] = piece
        end = len(targets) + len(names)
        self.put(names, got[len(targets) : end])
        return got[end:]

    def crosses(self, flow, also=(), cores=True):
        extra = []
        for level in range(2, len(self.order) + 1):
            extra += self.cross(flow, level, also if level == 2 else (), cores)
        return extra


def places_of(order):
    places = [0]
    for bit in reversed(order):
        places = places + [place | (1 << bit) for place in places]
    return places


def sum_kernel(shared, each, table, turned, upper, lower, *refs):
    outs = refs[shared + 2 * each :]
    half = upper.shape[0]
    total = matmul(turned[:, :half], upper[...]) + matmul(turned[:, half:], lower[...])
    for part in refs[:shared]:
        total = total + part[...].astype(jnp.float32)
    sides = 2 if len(outs) == 2 or each else 1
    for side in range(sides):

        @pl.when(pl.program_id(0) == side)
        def _(side=side):
            mine = total
            for part in refs[shared + side * each : shared + (side + 1) * each]:
                mine = mine + part[...].astype(jnp.float32)
            out = outs[side % len(outs)]
            out[...] = mine.astype(out.dtype)


def summed_rows(turned, right, rows, shared=(), parts=((), ()), apart=False):
    sides, count = len(rows), len(rows[0])
    tokens, columns = right.shape[0], right.shape[1] // sides
    block = turned.shape[0] // lax.axis_size("dp")
    table = [[place for side in rows for place in side]]
    table += [[places.index(place) for side in rows for place in side] for _, places in shared]
    for side in range(sides):
        table += [[places.index(place) for place in rows[side]] * sides for _, places in parts[side]]
    spots = jnp.array(table, jnp.int32)
    spots = spots.at[0].set(lax.bitwise_xor(spots[0], lax.axis_index("dp")))
    each = len(parts[0])

    def shared_spec(line):
        return pl.BlockSpec(
            (block, columns),
            lambda now, step, spots: (spots[line, now * count + step], now),
        )

    def one_side(side, row):
        def index(now, step, spots):
            step = jnp.where(now == side, step, jnp.where(now < side, 0, count - 1))
            return (row(step, spots), 0)

        return pl.BlockSpec((block, columns), index)

    def part_spec(side, line):
        return one_side(side, lambda step, spots: spots[line, step])

    if apart:
        out_shape = [jax.ShapeDtypeStruct((count * block, columns), jnp.bfloat16)] * sides
        out_specs = [one_side(side, lambda step, spots: step) for side in range(sides)]
    else:
        out_shape = [jax.ShapeDtypeStruct((count * block, sides * columns), jnp.bfloat16)]
        out_specs = [pl.BlockSpec((block, columns), lambda now, step, spots: (step, now))]
    base = 1 + len(shared)
    return pl.pallas_call(
        functools.partial(sum_kernel, len(shared), each),
        out_shape=out_shape,
        grid_spec=pltpu.PrefetchScalarGridSpec(
            num_scalar_prefetch=1,
            grid=(sides, count),
            in_specs=[
                pl.BlockSpec(
                    (block, tokens),
                    lambda now, step, spots: (spots[0, now * count + step], 0),
                ),
                pl.BlockSpec((tokens // 2, columns), lambda now, step, spots: (0, now)),
                pl.BlockSpec((tokens // 2, columns), lambda now, step, spots: (1, now)),
            ]
            + [shared_spec(1 + number) for number in range(len(shared))]
            + [
                part_spec(side, base + side * each + number)
                for side in range(sides)
                for number in range(each)
            ],
            out_specs=out_specs,
        ),
        **kernel_params(
            2 * tokens * sides * count * block * columns,
            2 * sides * count * block * columns * (1 + len(shared) + each),
        ),
    )(spots, turned, right, right, *[part for part, _ in shared], *[p for side in parts for p, _ in side])


class Pair:
    def __init__(self, turned, right, order):
        self.turned, self.right = turned, right
        self.orders = (order, order[::-1])
        self.kept = [places_of(turn) for turn in self.orders]
        self.whole = places_of(order)
        self.shared, self.parts, self.step = [], ([], []), 0

    def first(self):
        places = [place | 1 for place in self.whole]
        self.sent = summed_rows(self.turned, self.right, [places])
        return self.sent[0]

    def first_move(self):
        return (self.sent[0], 0)

    def first_receive(self, got):
        self.shared = [(got, self.whole)]

    def send(self):
        half = len(self.kept[0]) // 2
        self.sent = summed_rows(
            self.turned,
            self.right,
            [kept[half:] for kept in self.kept],
            self.shared,
            self.parts,
            apart=True,
        )
        self.kept = [kept[:half] for kept in self.kept]
        return self.sent

    def moves(self):
        return [(sent, turn[self.step]) for sent, turn in zip(self.sent, self.orders)]

    def receive(self, got):
        for piece, parts, kept in zip(got, self.parts, self.kept):
            parts.append((piece, kept))
        self.step += 1

    def left(self):
        return len(self.orders[0]) - self.step

    def line(self):
        self.sent = summed_rows(self.turned, self.right, self.kept, self.shared, self.parts)
        return self.sent[0]


def finish(line):
    return lax.psum_scatter(line, "seq", scatter_dimension=0, tiled=True).astype(jnp.float32)


class Halved:
    def __init__(self, blocks, order):
        self.order, self.step = order, 0
        self.kept = [block.astype(jnp.float32) for block in blocks]

    def left(self):
        return len(self.order) - self.step

    def moves(self):
        half = len(self.kept) // 2
        sent = jnp.concatenate(self.kept[half:], axis=0).astype(jnp.bfloat16)
        self.kept = self.kept[:half]
        return [(sent, self.order[self.step])]

    def receive(self, got):
        (got,) = got
        rows = got.shape[0] // len(self.kept)
        self.kept = [
            kept + got[number * rows : (number + 1) * rows].astype(jnp.float32)
            for number, kept in enumerate(self.kept)
        ]
        self.step += 1


def on_device(
    tokens,
    lengths,
    gain_one,
    w_query,
    w_key,
    w_value,
    w_out,
    gain_two,
    w_gate,
    w_up,
    w_down,
    cotangent,
):
    half_type = jnp.bfloat16
    batch, group, width = tokens.shape
    count = batch * group
    upper = tuple(range(1, dp_bits()))
    inner = w_query.shape[1]
    middle = w_down.shape[1] // 2

    def along(shard):
        return lax.all_gather(shard, "seq", axis=0, tiled=True)

    gains = jnp.stack([gain_one, gain_two], axis=1)
    first = jnp.concatenate(
        [w_query, w_key, w_value, jnp.pad(gains, ((0, 0), (0, HEAD - 2)))], axis=1
    ).astype(half_type)
    columns_first = inner + 2 * HEAD
    flow = Flow()
    line_first = along(first)
    line_out = along(after(w_out.astype(half_type), line_first))
    one_spread, two_spread, three_spread = Spreads(upper), Spreads(upper), Spreads(upper)
    one_spread.direct(flow, 0, line_first)
    line_gate = along(after(w_gate.astype(half_type), line_out, flow.ended))
    line_up = along(after(w_up.astype(half_type), line_gate))
    down_half = w_down.astype(half_type)
    quarter = middle + middle // 2
    line_right = along(after(down_half[:, middle:], line_up))
    early_spread = Shallow(down_half[:, :middle], upper)
    flow.holds(line_out)
    early_spread.put(one_spread.direct(flow, 1, line_out, early_spread.moves()))
    one_spread.crosses(flow)
    flow.holds(line_gate)
    left_over = one_spread.double()
    one_spread.put(
        left_over, two_spread.direct(flow, 0, line_gate, one_spread.moves(left_over))
    )
    full_one = one_spread.helds

    reach = (WINDOW - 2) // group + 1
    offset = lax.axis_index("seq") * group
    query_at = offset + jnp.arange(group, dtype=jnp.int32)
    key_at = offset - reach * group + jnp.arange((reach + 1) * group, dtype=jnp.int32)
    query_seg, query_pos = documents(lengths, query_at)
    key_seg = documents(lengths, key_at)[0]
    allowed = (
        (key_at[None, :] >= 0)
        & (query_at[:, None] >= key_at[None, :])
        & (query_at[:, None] - key_at[None, :] < WINDOW)
    )
    allowed = allowed & (query_seg[0][:, None] == key_seg[0][None, :])
    bias = jnp.where(allowed.T, 0.0, -1e30)
    cosine, sine = rope_tables(query_pos)
    rows = tokens.astype(jnp.float32).reshape(count, width)
    scale_one = lax.rsqrt(jnp.mean(rows * rows, axis=-1, keepdims=True) + EPS)
    mapped, normed, gain_rows = by_rows(rows * scale_one, full_one[0], columns_first)
    gain_a, gain_b = gain_rows[0], gain_rows[1]
    query = mapped[:, :inner].reshape(batch, group, HEADS, HEAD)
    key = mapped[:, inner : inner + HEAD].reshape(batch, group, HEAD)
    value = mapped[:, inner + HEAD :].astype(half_type).reshape(batch, group, HEAD)
    query_turned = rotate(query, cosine[:, :, None, :], sine[:, :, None, :]).astype(half_type)
    key_turned = rotate(key, cosine, sine).astype(half_type)
    paired = jnp.concatenate([key_turned, value], axis=-1)
    pieces = []
    for step in range(reach, 0, -1):
        pieces.append(shifted(paired, "seq", step))
    pieces.append(paired)
    seen = jnp.concatenate(pieces, axis=1)
    keys_seen = seen[..., :HEAD]
    values_seen = seen[..., HEAD:]

    query_turned = query_turned.reshape(count, HEADS * HEAD)
    keys_seen, values_seen = keys_seen[0], values_seen[0]
    flow.holds(line_up, query_turned)
    early_spread.put(two_spread.direct(flow, 1, line_up, early_spread.moves()))
    while early_spread.left():
        early_spread.put(flow.round(early_spread.moves()))
    places = sorted(early_spread.pieces)
    early = jnp.stack([early_spread.pieces[place] for place in places])
    early = lax.all_gather(after(early, line_right), "seq", axis=1, tiled=True)
    mixed, log_total = attend(bias, query_turned, keys_seen, values_seen.T)
    mid = rows + by_rows(mixed, full_one[1], width)[0]
    scale_two = lax.rsqrt(jnp.mean(mid * mid, axis=-1, keepdims=True) + EPS)
    normed_two = (mid * scale_two * gain_b).astype(half_type)

    turned_one, turned_mixed, turned_two = map(turned_over, (normed, mixed, normed_two))
    flow.holds(normed_two, line_right, turned_one, turned_mixed, turned_two)
    two_spread.crosses(flow)
    left_over = two_spread.double()
    lines_three = [line_right[:, : quarter - middle], line_right[:, quarter - middle :]]
    got = flow.round(two_spread.moves(left_over) + [(line, 0) for line in lines_three])
    two_spread.put(left_over, got)
    for held, piece in zip(three_spread.helds, got[len(left_over) :]):
        held[1] = piece
    full_two = two_spread.helds
    three_spread.both(flow, lines_three)
    order = Order()
    gate, up_val, hidden, hidden_turned = order(
        lambda left: gate_up(left, *full_two), normed_two
    )

    grad_out = cotangent.reshape(count, width)
    flow.holds(order.last)
    early = [early] + three_spread.crosses(flow, [(early, 0)], False)
    job_down = Pair(hidden_turned, grad_out, upper)
    order.first(job_down)
    flow.holds(order.last)
    left_over = three_spread.double()
    three_spread.put(left_over, flow.round(three_spread.moves(left_over)))
    job_down.first_receive(partner(after(job_down.sent[0], flow.ended), 0))
    full_three = three_spread.helds
    grad_gate, grad_up = order(
        lambda *operands: with_down(operands, early, full_three, True), gate, up_val, grad_out
    )
    job_gate = Pair(turned_two, grad_gate, upper)
    job_up = Pair(turned_two, grad_up, upper)

    def rest(job):
        while job.left() > 1:
            order.send(job)
            exchange(flow, [job])

    order.first(job_gate)
    job_gate.first_receive(partner(*job_gate.first_move()))
    order.first(job_up)
    job_down.right = after(job_down.right, order.last)
    order.last = summed_rows(job_down.turned, job_down.right, [job_down.whole], job_down.shared)
    down_parts = lax.psum_scatter(
        order.last[0].reshape(len(places), -1, width), "seq", scatter_dimension=1, tiled=True
    )
    sums = []
    for turn, part in (
        (upper, down_parts[:, :, :middle]),
        (upper[::-1], down_parts[:, :, middle:]),
    ):
        sums.append(Halved([part[job_down.whole.index(place)] for place in places_of(turn)], turn))
    order.send(job_gate)
    flow.holds(order.last)
    job_up.first_receive(exchange(flow, [job_gate], [job_up.first_move()])[0])

    grad_normed_two = order(
        lambda *lefts: back_by_rows(lefts, full_two, jnp.float32), grad_gate, grad_up
    )
    back_mid, gain_two_term = norm_back(grad_normed_two, mid, scale_two, gain_b)
    grad_mid = grad_out.astype(jnp.float32) + back_mid
    grad_branch = grad_mid.astype(half_type)
    job_out = Pair(turned_mixed, grad_branch, upper)
    order.last = [grad_branch]
    order.first(job_out)
    order.send(job_up)
    flow.holds(order.last)
    job_out.first_receive(exchange(flow, [job_up], [job_out.first_move()])[0])

    rest(job_gate)
    order.send(job_gate)
    grad_mixed = order(lambda left: back_by_rows([left], full_one[1:], half_type), grad_branch)
    grad_q, grad_keys, grad_values = order(
        lambda left: attend_back(
            bias, cosine[0].T, sine[0].T, query_turned, left, log_total, keys_seen, values_seen
        ),
        grad_mixed,
    )
    flow.holds(order.last)
    exchange(flow, [job_gate])

    grad_seen = jnp.concatenate([grad_keys, grad_values], axis=-1)[None]
    own, arrived = grad_seen[:, reach * group :], []
    for step in range(1, reach + 1):
        part = grad_seen[:, (reach - step) * group : (reach - step + 1) * group]
        part = shifted(part.astype(jnp.bfloat16), "seq", -step)
        arrived.append(part)
        own = own + part.astype(own.dtype)
    grad_key = rotate(own[..., :HEAD], cosine, -sine).astype(half_type).reshape(count, HEAD)
    grad_value = own[..., HEAD:].astype(half_type).reshape(count, HEAD)
    rest(job_up)
    order.send(job_up)
    output = order(
        lambda *operands: with_down(operands, early, full_three, False), hidden, mid
    ).reshape(batch, group, width)
    flow.holds(order.last)
    exchange(flow, [job_up])

    gate_done = finish(order.line(job_gate))
    grad_first = jnp.concatenate([grad_q, grad_key, grad_value], axis=1)
    job_first = Pair(turned_one, grad_first, upper)
    order.first(job_first)
    job_first.first_receive(partner(*job_first.first_move()))
    order.send(job_out)
    flow.holds(order.last)
    exchange(flow, [job_out])

    up_done = finish(order.line(job_up))
    order.send(job_first)
    flow.holds(order.last, down_parts)
    exchange(flow, [job_first])

    rest(job_out)
    order.send(job_out)
    grad_normed = order(
        lambda left: back_by_rows([left], full_one[:1], jnp.float32), grad_first
    )
    flow.holds(order.last)
    exchange(flow, [job_out])

    rest(job_first)
    order.send(job_first)
    flow.holds(order.last)
    exchange(flow, [job_first])
    grad_normed = after(grad_normed, flow.fence)
    back_rows, gain_one_term = norm_back(grad_normed, rows, scale_one, gain_a)
    grad_rows = (grad_mid + back_rows).astype(half_type).reshape(batch, group, width)
    gain_terms = jnp.stack([gain_one_term, gain_two_term])

    out_done = finish(order.line(job_out))
    first_done = finish(order.line(job_first))
    flow.holds(order.last)
    while sums[0].left():
        exchange(flow, sums)
    down_done = jnp.concatenate([part.kept[0] for part in sums], axis=1)
    bits = range(dp_bits())
    for bit in bits:
        gain_terms = gain_terms + partner(gain_terms, bit)
    gain_terms = sum(
        [around(gain_terms, steps) for steps in range(1, lax.axis_size("seq"))], gain_terms
    )
    owned = gain_one.shape[0]
    mine = (lax.axis_index("dp") * lax.axis_size("seq") + lax.axis_index("seq")) * owned
    gain_done = lax.dynamic_slice_in_dim(gain_terms, mine, owned, 1)
    return (
        output,
        grad_rows,
        gain_done[0],
        first_done[:, :inner],
        first_done[:, inner : inner + HEAD],
        first_done[:, inner + HEAD :],
        out_done,
        gain_done[1],
        gate_done,
        up_done,
        down_done,
    )


def solution(mesh):
    in_specs = (
        P("dp", "seq", None),
        P("dp", None),
        P(("dp", "seq")),
        P(("dp", "seq"), None),
        P(("dp", "seq"), None),
        P(("dp", "seq"), None),
        P(("dp", "seq"), None),
        P(("dp", "seq")),
        P(("dp", "seq"), None),
        P(("dp", "seq"), None),
        P(("dp", "seq"), None),
        P("dp", "seq", None),
    )
    out_specs = (
        P("dp", "seq", None),
        P("dp", "seq", None),
        P(("dp", "seq")),
        P(("dp", "seq"), None),
        P(("dp", "seq"), None),
        P(("dp", "seq"), None),
        P(("dp", "seq"), None),
        P(("dp", "seq")),
        P(("dp", "seq"), None),
        P(("dp", "seq"), None),
        P(("dp", "seq"), None),
    )
    return jax.shard_map(
        on_device, mesh=mesh, in_specs=in_specs, out_specs=out_specs, check_vma=False
    )
```
